256 devices in a mesh: row: 8 (over y, core), tm: 32 (over x, z).
Axes of the slice: x: 4, y: 4, z: 8, core: 2. Of those that a mesh axis runs over, the one named last changes fastest.
Arguments:
- residual: float32 [128, 1024, 1024], P('tm', 'row'), may hold values from -40 to 40, as said below
- direction: float32 [128, 1024, 1024], P('tm', 'row'), may hold values from -40 to 40, as said below
- observed: int32 [128, 1024, 1024], P('tm', 'row'), may hold values 0 or 1
- obs_weight: float32 [1024, 1024], P('row'), may hold values from 0.5 to 8
- ocean_blocks: int32 [128, 128], replicated, may hold values 0 or 1
- previous_dot: float32 [1], replicated, may hold values from 1 to 8
Outputs:
- residual_new: float32 [128, 1024, 1024], P('tm', 'row')
- precond: float32 [128, 1024, 1024], P('tm', 'row')
The draws below stay inside these ranges and needn't reach their ends.
Inputs may be any that keep to these rules, and one draw needn't show every extreme that they name: `residual`: a rough field whose magnitude varies by rows and hours over about two decades. `direction`: a rough field whose magnitude varies by rows and hours over about two decades.
All inputs are finite; a program needn't handle non-finite values. No bound on the sum of `observed` on one device may be relied on, other than what follows from the above.
Results may differ from the reference program's by a relative error of at most 0.0003.
Values sent between devices are 32-bit elements; how exact they have to be, the bound alone decides.
A program may use at most 192 MiB of HBM per device.

```python
import math
import jax
import jax.numpy as jnp
from jax import lax

NX = 1024
NY = 1024
NT = 128
BLOCK = 8


def scaled_field(key):
    keys = jax.random.split(key, 4)
    trend_rows = jnp.arange(NX, dtype=jnp.float32) / NX
    trend_hours = jnp.arange(NT, dtype=jnp.float32) / NT
    row_level = 0.5 * trend_rows + 0.5 * jax.random.uniform(keys[0], (NX,), dtype=jnp.float32)
    hour_level = 0.5 * trend_hours + 0.5 * jax.random.uniform(keys[1], (NT,), dtype=jnp.float32)
    row_scale = jnp.exp(math.log(10.0) * (row_level - 0.5))
    hour_scale = jnp.exp(math.log(10.0) * (hour_level - 0.5))
    base = jax.random.truncated_normal(keys[3], -4.0, 4.0, (NT, NX, NY), dtype=jnp.float32)
    return base * hour_scale[:, None, None] * row_scale[None, :, None]


def draw_residual(key, part):
    return scaled_field(jax.random.fold_in(key, 11))


def draw_direction(key, part):
    return scaled_field(jax.random.fold_in(key, 23))


def with_ends(array, own_key, smallest, largest):
    spot = [jax.random.randint(jax.random.fold_in(own_key, axis), (), 0, length) for axis, length in enumerate(array.shape)]
    widest = array.shape.index(max(array.shape))
    beside = spot[:widest] + [(spot[widest] + 1) % array.shape[widest]] + spot[widest + 1:]
    return array.at[tuple(spot)].set(smallest).at[tuple(beside)].set(largest)


def block_levels(rng, extent, pieces, low, top_value):
    def one(axis_at, blocks):
        draws = jax.random.uniform(jax.random.fold_in(jax.random.fold_in(rng, 6), axis_at), (blocks,), jnp.float32, low / len(pieces), top_value / len(pieces))
        return jnp.repeat(jnp.exp(draws), extent[axis_at] // blocks).reshape((-1,) + (1,) * (len(extent) - axis_at - 1))

    loudness = one(*pieces[0])
    for cut in pieces[1:]:
        loudness = loudness * one(*cut)
    return loudness


def setup_inputs(seed: int = 0) -> dict:
    arg_keys = jax.random.split(jax.random.key(seed), 7)
    return {
        "residual": draw_residual(jax.random.fold_in(arg_keys[6], 71), 0),
        "direction": draw_direction(jax.random.fold_in(arg_keys[6], 71), 0),
        "observed": with_ends((jax.random.randint(arg_keys[2], (NT, NX, NY), 0, 2) < 1).astype(jnp.int32), jax.random.fold_in(arg_keys[2], 1), 0, 1),
        "obs_weight": jnp.clip(jnp.exp(math.log(8.0) - 2.7725887 * jax.random.uniform(arg_keys[3], (NX, NY), jnp.float32) ** block_levels(arg_keys[3], (NX, NY), ((0, 8),), -0.2, 0.2)), 0.5, 8.0),
        "ocean_blocks": with_ends((jax.random.randint(arg_keys[4], (NX // BLOCK, NY // BLOCK), 0, 4) < 3).astype(jnp.int32), jax.random.fold_in(arg_keys[4], 1), 0, 1),
        "previous_dot": jnp.clip(jnp.exp(jax.random.uniform(arg_keys[5], (1,), jnp.float32, math.log(1.0), math.log(8.0))), 1.0, 8.0),
    }


nugget = 0.25
coupling = 50.0
precond_shift = 0.5

def pivots(diagonal_extra, hour, total_hours):
    hour_value = jnp.asarray(hour).astype(jnp.float32)
    root = jnp.sqrt(diagonal_extra * diagonal_extra + 4.0 * diagonal_extra)
    larger = 0.5 * (diagonal_extra + 2.0 + root)
    ratio_log = -2.0 * jnp.log(larger)
    factor = (root - diagonal_extra) / (root + diagonal_extra)
    value = larger * (1.0 + factor * jnp.exp((hour_value + 1.0) * ratio_log)) / (1.0 + factor * jnp.exp(hour_value * ratio_log))
    return value - jnp.where(jnp.asarray(hour) == total_hours - 1, 1.0, 0.0)

def mode_diagonal(row_freq, col_freq, total_rows, total_cols):
    row_term = 2.0 * jnp.cos(row_freq.astype(jnp.float32) * (2.0 * math.pi / total_rows))
    col_term = 2.0 * jnp.cos(col_freq.astype(jnp.float32) * (2.0 * math.pi / total_cols))
    eigen = 4.0 - row_term[:, None] - col_term[None, :]
    return (precond_shift + eigen) / coupling

def time_solve(right_side, diagonal_extra, total_hours):
    hour_ids = jnp.arange(total_hours, dtype=jnp.int32)

    def forward(previous, inputs):
        slab, hour = inputs
        value = slab + previous / pivots(diagonal_extra, hour - 1, total_hours)
        return (value, value)
    _, eliminated = lax.scan(forward, jnp.zeros_like(right_side[0]), (right_side, hour_ids))

    def backward(later, inputs):
        value, hour = inputs
        result = (value + later) / pivots(diagonal_extra, hour, total_hours)
        return (result, result)
    _, solved = lax.scan(backward, jnp.zeros_like(right_side[0]), (eliminated, hour_ids), reverse=True)
    return solved

def reference(residual, direction, observed, obs_weight, ocean_blocks, previous_dot):
    ocean = jnp.repeat(jnp.repeat(ocean_blocks, BLOCK, axis=0), BLOCK, axis=1).astype(jnp.float32)
    ocean_pad = jnp.pad(ocean, ((1, 1), (0, 0)))
    north_link = ocean * ocean_pad[:-2]
    south_link = ocean * ocean_pad[2:]
    east_link = ocean * jnp.roll(ocean, -1, axis=1)
    west_link = ocean * jnp.roll(ocean, 1, axis=1)

    def spatial_hour(inputs):
        field, seen = inputs
        padded = jnp.pad(field, ((1, 1), (0, 0)))
        north = padded[:-2]
        south = padded[2:]
        east = jnp.roll(field, -1, axis=1)
        west = jnp.roll(field, 1, axis=1)
        weight = seen.astype(jnp.float32) * ocean * obs_weight + nugget
        spatial = north_link * (field - north) + south_link * (field - south) + east_link * (field - east) + west_link * (field - west)
        return weight * field + spatial
    local_part = lax.map(spatial_hour, (direction, observed))
    differences = direction[1:] - direction[:-1]
    zero_slab = jnp.zeros_like(direction[:1])
    temporal = jnp.concatenate([zero_slab, differences], axis=0) - jnp.concatenate([differences, zero_slab], axis=0)
    image = local_part + coupling * temporal
    alpha = previous_dot[0] / jnp.mean(direction * image)
    residual_new = residual - alpha * image
    spectrum = jnp.fft.fft2(residual_new, axes=(1, 2))
    diagonal_extra = mode_diagonal(jnp.arange(NX, dtype=jnp.int32), jnp.arange(NY, dtype=jnp.int32), NX, NY)
    real_part = time_solve(jnp.real(spectrum), diagonal_extra, NT)
    imag_part = time_solve(jnp.imag(spectrum), diagonal_extra, NT)
    precond = jnp.real(jnp.fft.ifft2(lax.complex(real_part, imag_part), axes=(1, 2)))
    return (residual_new, precond)
```

```python
import functools
import math

import jax
import jax.numpy as jnp
import ml_dtypes
import numpy as np
from jax import lax
from jax.experimental import pallas as pl
from jax.experimental.pallas import tpu as pltpu
from jax.sharding import PartitionSpec as P

MESH = pl.DeviceIdType.MESH
BF16 = jnp.bfloat16
F32 = jnp.float32

BLOCK = 8
NUGGET = 0.25
COUPLING = 50.0
PRECOND_SHIFT = 0.5

N = 1024
NT = 128
ROWS = 8
TM = 32
HOURS = NT // TM
BAND = N // ROWS
CHUNKS = 4
CK = BAND // CHUNKS
M = HOURS * CK
FRONT = HOURS * BAND

NN = (((1,), (0,)), ((), ()))
NT_DIMS = (((1,), (1,)), ((), ()))


def split_np(table):
    high = table.astype(ml_dtypes.bfloat16)
    low = (table - high.astype(np.float64)).astype(ml_dtypes.bfloat16)
    return np.stack([high, low])


def tables():
    def cas(freq, count):
        phase = (freq[:, None] * np.arange(count)[None, :]) % N
        angle = phase * (2.0 * math.pi / N)
        return np.cos(angle) + np.sin(angle)

    four = 4 * np.arange(N // 4)
    two = four + 2
    odd = 2 * np.arange(N // 2) + 1
    even_table = np.stack([split_np(cas(four, N // 4)), split_np(cas(two, N // 4))])
    odd_table = split_np(cas(odd, N // 2))
    order = np.concatenate([four, two, odd])
    lam = (2.0 - 2.0 * np.cos(order * (2.0 * math.pi / N))).astype(np.float32)
    lam_rows = np.broadcast_to(lam.reshape(8, 1, 128), (8, 8, 128)).copy()
    lam_cols = np.broadcast_to(lam[:, None], (N, 128)).copy()
    return even_table, odd_table, lam_rows, lam_cols


def dot3(a_hi, a_lo, b_hi, b_lo, dims):
    def one(a, b):
        return lax.dot_general(a, b, dims, preferred_element_type=F32)

    return one(a_hi, b_hi) + (one(a_hi, b_lo) + one(a_lo, b_hi))


def split(value):
    high = value.astype(BF16)
    low = (value - high.astype(F32)).astype(BF16)
    return high, low


def decay(eigen):
    a = (PRECOND_SHIFT + eigen) * (1.0 / COUPLING)
    root = jnp.sqrt(a * a + 4.0 * a)
    return 2.0 / (a + 2.0 + root)


def freq_start(row, chunk):
    odd = row // 4
    even = 1 - odd
    half = (row // 2) % 2
    start = odd * (512 + chunk * (4 * CK) + (row - 4) * CK) + even * (
        half * 256 + chunk * (2 * CK) + (row % 2) * CK
    )
    return pl.multiple_of(start, CK)


def solve_kernel(
    res, te, to, lam_rows, lam_cols, y,
    r_even, r_odd, v_even, v_odd, send_a, recv_a, spec, fg, own, back, inc, send_w,
    sem_sa, sem_ra, sem_sf, sem_rf, sem_sb, sem_rb, sem_sw, sem_rw,
):
    row = lax.axis_index("row")
    tm = lax.axis_index("tm")

    barrier = pltpu.get_barrier_semaphore()

    @pl.loop(1, ROWS)
    def _(o):
        pl.semaphore_signal(
            barrier, inc=1, device_id={"row": lax.rem(row + o, ROWS)}, device_id_type=MESH
        )

    @pl.loop(1, TM)
    def _(o):
        pl.semaphore_signal(
            barrier, inc=1, device_id={"tm": lax.rem(tm + o, TM)}, device_id_type=MESH
        )

    for h in range(HOURS):
        rows = slice(h * BAND, (h + 1) * BAND)
        low = res[rows, 0:512]
        high = res[rows, 512:1024]
        hi, lo = split(low - high)
        r_odd[0, rows, :] = hi
        r_odd[1, rows, :] = lo
        even = low + high
        for s, value in ((0, even[:, :256] + even[:, 256:]), (1, even[:, :256] - even[:, 256:])):
            hi, lo = split(value)
            r_even[s, 0, rows, :] = hi
            r_even[s, 1, rows, :] = lo

    pl.semaphore_wait(barrier, ROWS - 1 + TM - 1)

    def stage_a(c):
        part = pl.ds(pl.multiple_of(c * (4 * CK), 4 * CK), 4 * CK)
        out = dot3(to[0, part, :], to[1, part, :], r_odd[0], r_odd[1], NT_DIMS)
        for r in range(4):
            send_a[c, 4 + r] = out[r * CK:(r + 1) * CK]
        part = pl.ds(pl.multiple_of(c * (2 * CK), 2 * CK), 2 * CK)
        for s in range(2):
            out = dot3(
                te[s, 0, part, :], te[s, 1, part, :], r_even[s, 0], r_even[s, 1], NT_DIMS
            )
            for r in range(2):
                send_a[c, 2 * s + r] = out[r * CK:(r + 1) * CK]
        recv_a[c, row] = send_a[c, row]

        @pl.loop(1, ROWS)
        def _(o):
            peer = lax.rem(row + o, ROWS)
            pltpu.make_async_remote_copy(
                src_ref=send_a.at[c, peer],
                dst_ref=recv_a.at[c, row],
                send_sem=sem_sa.at[c],
                recv_sem=sem_ra.at[c],
                device_id={"row": peer},
                device_id_type=MESH,
            ).start()

    def wait_for(ref, sem):
        pltpu.make_async_copy(ref, ref, sem).wait()

    def stage_b(c):
        wait_for(recv_a.at[c, pl.ds(0, ROWS - 1)], sem_ra.at[c])
        for h in range(HOURS):
            rows = slice(h * CK, (h + 1) * CK)
            lanes = slice(h * BAND, (h + 1) * BAND)
            v = [recv_a[c, r, :, lanes] for r in range(ROWS)]
            e = [v[r] + v[r + 4] for r in range(4)]
            for r in range(4):
                hi, lo = split(v[r] - v[r + 4])
                v_odd[0, rows, r * BAND:(r + 1) * BAND] = hi
                v_odd[1, rows, r * BAND:(r + 1) * BAND] = lo
            for r in range(2):
                for s, value in ((0, e[r] + e[r + 2]), (1, e[r] - e[r + 2])):
                    hi, lo = split(value)
                    v_even[s, 0, rows, r * BAND:(r + 1) * BAND] = hi
                    v_even[s, 1, rows, r * BAND:(r + 1) * BAND] = lo
        spec[c, :, 512:1024] = dot3(v_odd[0], v_odd[1], to[0], to[1], NT_DIMS)
        for s in range(2):
            spec[c, :, s * 256:(s + 1) * 256] = dot3(
                v_even[s, 0], v_even[s, 1], te[s, 0], te[s, 1], NT_DIMS
            )

    def chunk_decay(c, q):
        start = pl.multiple_of(freq_start(row, c) + q * 8, 8)
        col = lam_cols[pl.ds(start, 8), :]
        return jnp.concatenate([decay(lam_rows[l] + col) for l in range(8)], axis=1)

    def stage_c(c):
        for q in range(CK // 8):
            rho = chunk_decay(c, q)
            b = [spec[c, h * CK + q * 8:h * CK + q * 8 + 8, :] for h in range(HOURS)]
            f = b[3] + rho * (b[2] + rho * (b[1] + rho * b[0]))
            g = b[0] + rho * (b[1] + rho * (b[2] + rho * b[3]))
            for l in range(8):
                fg[c, q * 8 + l, 0:8, :] = f[:, l * 128:(l + 1) * 128]
                fg[c, q * 8 + l, 8:16, :] = g[:, l * 128:(l + 1) * 128]
        own[c, tm] = fg[c, tm]

        @pl.loop(1, TM)
        def _(o):
            peer = lax.rem(tm + o, TM)
            pltpu.make_async_remote_copy(
                src_ref=fg.at[c, peer],
                dst_ref=own.at[c, tm],
                send_sem=sem_sf.at[c],
                recv_sem=sem_rf.at[c],
                device_id={"tm": peer},
                device_id_type=MESH,
            ).start()

    def stage_d(c):
        wait_for(own.at[c, pl.ds(0, TM - 1)], sem_rf.at[c])
        start = pl.multiple_of(freq_start(row, c) + (tm // 8) * 8, 8)
        rho = decay(lam_rows[tm % 8] + lam_cols[pl.ds(start, 8), :])
        rho2 = rho * rho
        rho4 = rho2 * rho2
        whole = rho4
        for _ in range(5):
            whole = whole * whole
        zero = jnp.zeros((8, 128), F32)

        def sums(d, carry):
            p, q = carry
            return own[c, d, 0:8, :] + rho4 * p, own[c, TM - 1 - d, 8:16, :] + rho4 * q

        right, left = lax.fori_loop(0, TM, sums, (zero, zero), unroll=8)
        scale = 1.0 / (1.0 - whole * whole)
        p = (left + whole * right) * scale
        q = (right + whole * left) * scale

        def starts(d, carry):
            p, q = carry
            back[c, d, 0:8, :] = p
            back[c, TM - 1 - d, 8:16, :] = q
            return own[c, d, 0:8, :] + rho4 * p, own[c, TM - 1 - d, 8:16, :] + rho4 * q

        lax.fori_loop(0, TM, starts, (p, q), unroll=8)
        inc[c, tm] = back[c, tm]

        @pl.loop(1, TM)
        def _(o):
            peer = lax.rem(tm + o, TM)
            pltpu.make_async_remote_copy(
                src_ref=back.at[c, peer],
                dst_ref=inc.at[c, tm],
                send_sem=sem_sb.at[c],
                recv_sem=sem_rb.at[c],
                device_id={"tm": peer},
                device_id_type=MESH,
            ).start()

    def stage_e(c):
        wait_for(inc.at[c, pl.ds(0, TM - 1)], sem_rb.at[c])
        for q in range(CK // 8):
            rho = chunk_decay(c, q)
            f = jnp.concatenate([inc[c, q * 8 + l, 0:8, :] for l in range(8)], axis=1)
            g = jnp.concatenate([inc[c, q * 8 + l, 8:16, :] for l in range(8)], axis=1)
            scale = rho / (1.0 - rho * rho) * (1.0 / float(N * N))
            b = [spec[c, h * CK + q * 8:h * CK + q * 8 + 8, :] for h in range(HOURS)]
            later = [None] * HOURS
            g = rho * g
            for h in range(HOURS - 1, -1, -1):
                later[h] = g
                if h:
                    g = rho * (b[h] + g)
            for h in range(HOURS):
                f = b[h] + rho * f
                spec[c, h * CK + q * 8:h * CK + q * 8 + 8, :] = scale * (f + later[h])

    def stage_f(c):
        hi, lo = split(spec[c, :, 512:1024])
        odd = dot3(hi, lo, to[0], to[1], NN)
        parts = []
        for s in range(2):
            hi, lo = split(spec[c, :, s * 256:(s + 1) * 256])
            parts.append(dot3(hi, lo, te[s, 0], te[s, 1], NN))
        even = jnp.concatenate([parts[0] + parts[1], parts[0] - parts[1]], axis=1)
        for half, value in ((0, even + odd), (1, even - odd)):
            for r in range(4):
                for h in range(HOURS):
                    send_w[c, 4 * half + r, :, h * BAND:(h + 1) * BAND] = value[
                        h * CK:(h + 1) * CK, r * BAND:(r + 1) * BAND
                    ]
        here = pl.ds(freq_start(row, c), CK)
        y[here, :] = send_w[c, row]

        @pl.loop(1, ROWS)
        def _(o):
            peer = lax.rem(row + o, ROWS)
            pltpu.make_async_remote_copy(
                src_ref=send_w.at[c, peer],
                dst_ref=y.at[here, :],
                send_sem=sem_sw.at[c],
                recv_sem=sem_rw.at[c],
                device_id={"row": peer},
                device_id_type=MESH,
            ).start()

    @pl.loop(0, CHUNKS)
    def _(c):
        stage_a(c)

    @pl.loop(0, CHUNKS + 2)
    def _(i):
        @pl.when(i < CHUNKS)
        def _():
            stage_b(i)
            stage_c(i)

        @pl.when((i >= 1) & (i < CHUNKS + 1))
        def _():
            stage_d(i - 1)

        @pl.when(i >= 2)
        def _():
            stage_e(i - 2)
            stage_f(i - 2)

    @pl.loop(0, CHUNKS)
    def _(c):
        wait_for(send_a.at[c, pl.ds(0, ROWS - 1)], sem_sa.at[c])
        wait_for(fg.at[c, pl.ds(0, TM - 1)], sem_sf.at[c])
        wait_for(back.at[c, pl.ds(0, TM - 1)], sem_sb.at[c])
        wait_for(send_w.at[c, pl.ds(0, ROWS - 1)], sem_sw.at[c])
        wait_for(send_w.at[c, pl.ds(0, ROWS - 1)], sem_rw.at[c])


def spectral_solve(res, te, to, lam_rows, lam_cols):
    vmem = pl.BlockSpec(memory_space=pltpu.VMEM)
    return pl.pallas_call(
        solve_kernel,
        out_shape=jax.ShapeDtypeStruct((N, FRONT), F32),
        in_specs=[vmem] * 5,
        out_specs=vmem,
        scratch_shapes=[
            pltpu.VMEM((2, 2, FRONT, 256), BF16),
            pltpu.VMEM((2, FRONT, 512), BF16),
            pltpu.VMEM((2, 2, M, 256), BF16),
            pltpu.VMEM((2, M, 512), BF16),
            pltpu.VMEM((CHUNKS, ROWS, CK, FRONT), F32),
            pltpu.VMEM((CHUNKS, ROWS, CK, FRONT), F32),
            pltpu.VMEM((CHUNKS, M, N), F32),
            pltpu.VMEM((CHUNKS, TM, 16, 128), F32),
            pltpu.VMEM((CHUNKS, TM, 16, 128), F32),
            pltpu.VMEM((CHUNKS, TM, 16, 128), F32),
            pltpu.VMEM((CHUNKS, TM, 16, 128), F32),
            pltpu.VMEM((CHUNKS, ROWS, CK, FRONT), F32),
        ]
        + [pltpu.SemaphoreType.DMA((CHUNKS,))] * 8,
        compiler_params=pltpu.CompilerParams(
            collective_id=1, has_side_effects=True, vmem_limit_bytes=48 * 1024 * 1024
        ),
        name="spectral_solve",
    )(res, te, to, lam_rows, lam_cols)


def finish_kernel(y, te, to, out):
    value = y[...].T
    hi, lo = split(value[:, 512:1024])
    odd = dot3(hi, lo, to[0], to[1], NN)
    parts = []
    for s in range(2):
        hi, lo = split(value[:, s * 256:(s + 1) * 256])
        parts.append(dot3(hi, lo, te[s, 0], te[s, 1], NN))
    even = jnp.concatenate([parts[0] + parts[1], parts[0] - parts[1]], axis=1)
    out[0, :, 0:512] = even + odd
    out[0, :, 512:1024] = even - odd


def finish(y, te, to):
    return pl.pallas_call(
        finish_kernel,
        grid=(HOURS,),
        out_shape=jax.ShapeDtypeStruct((HOURS, BAND, N), F32),
        in_specs=[
            pl.BlockSpec((N, BAND), lambda h: (0, h)),
            pl.BlockSpec((2, 2, 256, 256), lambda h: (0, 0, 0, 0)),
            pl.BlockSpec((2, 512, 512), lambda h: (0, 0, 0)),
        ],
        out_specs=pl.BlockSpec((1, BAND, N), lambda h: (h, 0, 0)),
        compiler_params=pltpu.CompilerParams(vmem_limit_bytes=48 * 1024 * 1024),
        name="finish",
    )(y, te, to)


def extended_2(block, sides, width):
    for axis, dim in sides:
        count = lax.axis_size(axis)
        forward = [(i, i + 1) for i in range(count - 1)]
        backward = [(target, source) for source, target in forward]
        low = lax.ppermute(
            lax.slice_in_dim(block, block.shape[dim] - width, None, axis=dim), axis, forward
        )
        high = lax.ppermute(lax.slice_in_dim(block, 0, width, axis=dim), axis, backward)
        block = jnp.concatenate([low, block, high], axis=dim)
    return block


def per_device(residual, direction, observed, obs_weight, ocean_blocks, previous_dot):
    hours, rows, cols = direction.shape
    row_index = lax.axis_index("row")
    hour_index = lax.axis_index("tm")
    row_count = lax.axis_size("row")
    hour_count = lax.axis_size("tm")
    total_hours = hours * hour_count
    total_rows = rows * row_count
    widened = jnp.repeat(ocean_blocks, BLOCK, axis=1).astype(jnp.float32)
    padded_blocks = jnp.pad(widened, ((1, 1), (0, 0)))
    cell_rows = jnp.repeat(padded_blocks, BLOCK, axis=0)
    ocean_rim = lax.dynamic_slice_in_dim(cell_rows, row_index * rows + BLOCK - 1, rows + 2, 0)
    ocean = ocean_rim[1:-1]
    north_link = ocean * ocean_rim[:-2]
    south_link = ocean * ocean_rim[2:]
    east_link = ocean * jnp.roll(ocean, -1, axis=1)
    west_link = ocean * jnp.roll(ocean, 1, axis=1)
    extended = extended_2(direction, (("row", 1), ("tm", 0)), 1)
    time_prev = extended[:-2, 1:-1]
    time_next = extended[2:, 1:-1]
    north = extended[1:-1, :-2]
    south = extended[1:-1, 2:]
    east = jnp.roll(direction, -1, axis=2)
    west = jnp.roll(direction, 1, axis=2)
    hour_ids = hour_index * hours + jnp.arange(hours, dtype=jnp.int32)
    has_prev = (hour_ids > 0).astype(jnp.float32)[:, None, None]
    has_next = (hour_ids < total_hours - 1).astype(jnp.float32)[:, None, None]
    temporal = has_prev * (direction - time_prev) + has_next * (direction - time_next)
    weight = observed.astype(jnp.float32) * ocean * obs_weight + NUGGET
    spatial = (
        north_link * (direction - north)
        + south_link * (direction - south)
        + east_link * (direction - east)
        + west_link * (direction - west)
    )
    image = weight * direction + spatial + COUPLING * temporal
    total_dot = lax.psum(jnp.sum(direction * image), ("row", "tm"))
    alpha = previous_dot[0] / (total_dot / float(total_hours * total_rows * cols))
    residual_new = residual - alpha * image
    te, to, lam_rows, lam_cols = (jnp.asarray(t) for t in tables())
    y = spectral_solve(residual_new.reshape(FRONT, N), te, to, lam_rows, lam_cols)
    precond = finish(y, te, to)
    return (residual_new, precond)


def solution(mesh):
    in_specs = (
        P("tm", "row", None),
        P("tm", "row", None),
        P("tm", "row", None),
        P("row", None),
        P(),
        P(),
    )
    out_specs = (P("tm", "row", None), P("tm", "row", None))
    return jax.shard_map(
        per_device, mesh=mesh, in_specs=in_specs, out_specs=out_specs, check_vma=False
    )
```

```python
import math

import jax
import jax.numpy as jnp
import ml_dtypes
import numpy as np
from jax import lax
from jax.experimental import pallas as pl
from jax.experimental.pallas import tpu as pltpu
from jax.sharding import PartitionSpec as P

MESH = pl.DeviceIdType.MESH
BF16 = jnp.bfloat16
F32 = jnp.float32

BLOCK = 8
NUGGET = 0.25
COUPLING = 50.0
PRECOND_SHIFT = 0.5

N = 1024
NT = 128
ROWS = 8
TM = 32
HOURS = NT // TM
BAND = N // ROWS
CHUNKS = 4
CK = BAND // CHUNKS
M = HOURS * CK
FRONT = HOURS * BAND

NN = (((1,), (0,)), ((), ()))
NT_DIMS = (((1,), (1,)), ((), ()))


def split_np(table):
    high = table.astype(ml_dtypes.bfloat16)
    low = (table - high.astype(np.float64)).astype(ml_dtypes.bfloat16)
    return np.stack([high, low])


def tables():
    def cas(freq, count):
        phase = (freq[:, None] * np.arange(count)[None, :]) % N
        angle = phase * (2.0 * math.pi / N)
        return np.cos(angle) + np.sin(angle)

    four = 4 * np.arange(N // 4)
    two = four + 2
    odd = 2 * np.arange(N // 2) + 1
    even_table = np.stack([split_np(cas(four, N // 4)), split_np(cas(two, N // 4))])
    odd_table = split_np(cas(odd, N // 2))
    order = np.concatenate([four, two, odd])
    lam = (2.0 - 2.0 * np.cos(order * (2.0 * math.pi / N))).astype(np.float32)
    lam_rows = np.broadcast_to(lam.reshape(8, 1, 128), (8, 8, 128)).copy()
    lam_cols = np.broadcast_to(lam[:, None], (N, 128)).copy()
    return even_table, odd_table, lam_rows, lam_cols


def dot3(a_hi, a_lo, b_hi, b_lo, dims):
    def one(a, b):
        return lax.dot_general(a, b, dims, preferred_element_type=F32)

    return one(a_hi, b_hi) + (one(a_hi, b_lo) + one(a_lo, b_hi))


def split(value):
    high = value.astype(BF16)
    low = (value - high.astype(F32)).astype(BF16)
    return high, low


def decay(eigen):
    a = (PRECOND_SHIFT + eigen) * (1.0 / COUPLING)
    root = jnp.sqrt(a * a + 4.0 * a)
    return 2.0 / (a + 2.0 + root)


def freq_start(row, chunk):
    odd = row // 4
    even = 1 - odd
    half = (row // 2) % 2
    start = odd * (512 + chunk * (4 * CK) + (row - 4) * CK) + even * (
        half * 256 + chunk * (2 * CK) + (row % 2) * CK
    )
    return pl.multiple_of(start, CK)


def step_kernel(
    direction, residual, observed, obs_weight, blocks, te_in, to_in, lam_rows_in, lam_cols_in, previous,
    y, res_out,
    dir_v, res_v, obs_v, wgt_v, blk_v, te, to, lam_rows, lam_cols,
    image, halo_t, halo_r, ocean, dots, dot_row, dot_z, dot_x,
    r_even, r_odd, v_even, v_odd, send_a, recv_a, spec, fg, own, back, inc, send_w,
    sem_in, sem_out, sem_hs, sem_hr, sem_ds, sem_dr,
    sem_sa, sem_ra, sem_sf, sem_rf, sem_sb, sem_rb, sem_sw, sem_rw,
):
    row = lax.axis_index("row")
    tm = lax.axis_index("tm")
    loads = [
        pltpu.make_async_copy(src, dst, sem_in.at[k])
        for k, (src, dst) in enumerate((
            (blocks, blk_v), (direction, dir_v), (obs_weight, wgt_v), (observed, obs_v),
            (residual, res_v), (te_in, te), (to_in, to), (lam_rows_in, lam_rows),
            (lam_cols_in, lam_cols),
        ))
    ]
    for load in loads:
        load.start()

    barrier = pltpu.get_barrier_semaphore()

    @pl.loop(1, ROWS)
    def _(o):
        pl.semaphore_signal(
            barrier, inc=1, device_id={"row": lax.rem(row + o, ROWS)}, device_id_type=MESH
        )

    @pl.loop(1, TM)
    def _(o):
        pl.semaphore_signal(
            barrier, inc=1, device_id={"tm": lax.rem(tm + o, TM)}, device_id_type=MESH
        )

    def remote(src, dst, send_sem, recv_sem, axis, peer):
        return pltpu.make_async_remote_copy(
            src_ref=src, dst_ref=dst, send_sem=send_sem, recv_sem=recv_sem,
            device_id={axis: peer}, device_id_type=MESH,
        )

    def wait_for(ref, sem):
        pltpu.make_async_copy(ref, ref, sem).wait()

    pl.semaphore_wait(barrier, ROWS - 1 + TM - 1)
    tm_next, tm_prev = lax.rem(tm + 1, TM), lax.rem(tm + TM - 1, TM)
    row_next, row_prev = lax.rem(row + 1, ROWS), lax.rem(row + ROWS - 1, ROWS)
    halos = [
        remote(direction.at[HOURS - 1], halo_t.at[0], sem_hs.at[0], sem_hr.at[0], "tm", tm_next),
        remote(direction.at[0], halo_t.at[1], sem_hs.at[1], sem_hr.at[1], "tm", tm_prev),
        remote(
            direction.at[:, pl.ds(BAND - 8, 8), :], halo_r.at[0], sem_hs.at[2], sem_hr.at[2],
            "row", row_next,
        ),
        remote(
            direction.at[:, pl.ds(0, 8), :], halo_r.at[1], sem_hs.at[3], sem_hr.at[3],
            "row", row_prev,
        ),
    ]
    for halo in halos:
        halo.start()

    loads[0].wait()
    spread = (
        lax.broadcasted_iota(jnp.int32, (N // BLOCK, N), 1) // BLOCK
        == lax.broadcasted_iota(jnp.int32, (N // BLOCK, N), 0)
    ).astype(F32).astype(BF16)
    ocean[0:8, :] = jnp.zeros((8, N), F32)
    ocean[136:144, :] = jnp.zeros((8, N), F32)
    ocean[8:136, :] = lax.dot_general(
        blk_v[...].astype(F32).astype(BF16), spread, NN, preferred_element_type=F32
    )
    for k in (1, 2, 3):
        loads[k].wait()

    sub = lax.broadcasted_iota(jnp.int32, (8, N), 0)

    def wide(i):
        return jnp.broadcast_to(ocean[pl.ds(row * (BAND // BLOCK) + i + 8, 1), :], (8, N))

    def strip(i, above, below, acc):
        here = pl.ds(pl.multiple_of(i * 8, 8), 8)
        sea, sea_up, sea_down = wide(i), wide(i - 1), wide(i + 1)
        north_link = sea * jnp.where(sub == 0, sea_up, sea)
        south_link = sea * jnp.where(sub == 7, sea_down, sea)
        east_link = sea * pltpu.roll(sea, N - 1, 1)
        sea_weight = sea * wgt_v[here, :]
        v = [dir_v[h, here, :] for h in range(HOURS)]
        for h in range(HOURS):
            north = jnp.where(sub == 0, pltpu.roll(above(h), 1, 0), pltpu.roll(v[h], 1, 0))
            south = jnp.where(sub == 7, pltpu.roll(below(h), 7, 0), pltpu.roll(v[h], 7, 0))
            flux = east_link * (v[h] - pltpu.roll(v[h], N - 1, 1))
            value = (obs_v[h, here, :].astype(F32) * sea_weight + NUGGET) * v[h]
            value += north_link * (v[h] - north) + south_link * (v[h] - south)
            value += flux - pltpu.roll(flux, 1, 1)
            near = [v[h] - v[k] for k in (h - 1, h + 1) if 0 <= k < HOURS]
            value += COUPLING * (near[0] + near[1] if len(near) == 2 else near[0])
            image[h, here, :] = value
            acc += value * v[h]
        return acc

    def inner(i, acc):
        above = pl.ds(pl.multiple_of(i * 8 - 8, 8), 8)
        below = pl.ds(pl.multiple_of(i * 8 + 8, 8), 8)
        return strip(i, lambda h: dir_v[h, above, :], lambda h: dir_v[h, below, :], acc)

    strips = BAND // 8
    acc = lax.fori_loop(1, strips - 1, inner, jnp.zeros((8, N), F32))
    wait_for(halo_r.at[0], sem_hr.at[2])
    acc = strip(0, lambda h: halo_r[0, h], lambda h: dir_v[h, 8:16, :], acc)
    wait_for(halo_r.at[1], sem_hr.at[3])
    acc = strip(
        strips - 1, lambda h: dir_v[h, BAND - 16:BAND - 8, :], lambda h: halo_r[1, h], acc
    )

    wait_for(halo_t.at[0], sem_hr.at[0])
    wait_for(halo_t.at[1], sem_hr.at[1])
    hour_links = (
        jnp.full((8, N), jnp.where(tm > 0, COUPLING, 0.0), F32),
        jnp.full((8, N), jnp.where(tm < TM - 1, COUPLING, 0.0), F32),
    )

    def outer(i, acc):
        here = pl.ds(pl.multiple_of(i * 8, 8), 8)
        for side, h in ((0, 0), (1, HOURS - 1)):
            v = dir_v[h, here, :]
            extra = hour_links[side] * (v - halo_t[side, here, :])
            image[h, here, :] += extra
            acc += extra * v
        return acc

    acc = lax.fori_loop(0, strips, outer, acc)

    tile = acc[:, 0:128]
    for l in range(1, 8):
        tile += acc[:, l * 128:(l + 1) * 128]

    def share(tile, k, buf, count, me, axis, peer_of):
        dots[k] = tile
        buf[me] = tile

        @pl.loop(1, count)
        def _(o):
            remote(
                dots.at[k], buf.at[me], sem_ds.at[k], sem_dr.at[k], axis, peer_of(o)
            ).start()

        wait_for(buf.at[pl.ds(0, count - 1)], sem_dr.at[k])
        total = buf[0]
        for j in range(1, count):
            total += buf[j]
        return total

    x, z = tm // 8, tm % 8
    tile = share(tile, 0, dot_row, ROWS, row, "row", lambda o: lax.rem(row + o, ROWS))
    tile = share(tile, 1, dot_z, 8, z, "tm", lambda o: x * 8 + lax.rem(z + o, 8))
    tile = share(tile, 2, dot_x, 4, x, "tm", lambda o: lax.rem(x + o, 4) * 8 + z)
    total = jnp.sum(jnp.sum(tile, axis=1, keepdims=True), axis=0, keepdims=True)
    alpha = previous[0] / (total / float(NT * N * N))

    for k in range(4, 9):
        loads[k].wait()
    for h in range(HOURS):
        @pl.loop(0, BAND // 16)
        def _(i):
            here = pl.ds(pl.multiple_of(i * 16, 16), 16)
            rows = pl.ds(pl.multiple_of(h * BAND + i * 16, 16), 16)
            value = res_v[h, here, :] - alpha * image[h, here, :]
            image[h, here, :] = value
            low = value[:, 0:512]
            high = value[:, 512:1024]
            hi, lo = split(low - high)
            r_odd[0, rows, :] = hi
            r_odd[1, rows, :] = lo
            even = low + high
            for s, part in ((0, even[:, :256] + even[:, 256:]), (1, even[:, :256] - even[:, 256:])):
                hi, lo = split(part)
                r_even[s, 0, rows, :] = hi
                r_even[s, 1, rows, :] = lo

    store = pltpu.make_async_copy(image, res_out, sem_out.at[0])
    store.start()

    def stage_a(c):
        part = pl.ds(pl.multiple_of(c * (4 * CK), 4 * CK), 4 * CK)
        out = dot3(to[0, part, :], to[1, part, :], r_odd[0], r_odd[1], NT_DIMS)
        for r in range(4):
            send_a[c, 4 + r] = out[r * CK:(r + 1) * CK]
        part = pl.ds(pl.multiple_of(c * (2 * CK), 2 * CK), 2 * CK)
        for s in range(2):
            out = dot3(
                te[s, 0, part, :], te[s, 1, part, :], r_even[s, 0], r_even[s, 1], NT_DIMS
            )
            for r in range(2):
                send_a[c, 2 * s + r] = out[r * CK:(r + 1) * CK]
        recv_a[c, row] = send_a[c, row]

        @pl.loop(1, ROWS)
        def _(o):
            peer = lax.rem(row + o, ROWS)
            pltpu.make_async_remote_copy(
                src_ref=send_a.at[c, peer],
                dst_ref=recv_a.at[c, row],
                send_sem=sem_sa.at[c],
                recv_sem=sem_ra.at[c],
                device_id={"row": peer},
                device_id_type=MESH,
            ).start()

    def stage_b(c):
        wait_for(recv_a.at[c, pl.ds(0, ROWS - 1)], sem_ra.at[c])
        for h in range(HOURS):
            rows = slice(h * CK, (h + 1) * CK)
            lanes = slice(h * BAND, (h + 1) * BAND)
            v = [recv_a[c, r, :, lanes] for r in range(ROWS)]
            e = [v[r] + v[r + 4] for r in range(4)]
            for r in range(4):
                hi, lo = split(v[r] - v[r + 4])
                v_odd[0, rows, r * BAND:(r + 1) * BAND] = hi
                v_odd[1, rows, r * BAND:(r + 1) * BAND] = lo
            for r in range(2):
                for s, value in ((0, e[r] + e[r + 2]), (1, e[r] - e[r + 2])):
                    hi, lo = split(value)
                    v_even[s, 0, rows, r * BAND:(r + 1) * BAND] = hi
                    v_even[s, 1, rows, r * BAND:(r + 1) * BAND] = lo
        spec[c, :, 512:1024] = dot3(v_odd[0], v_odd[1], to[0], to[1], NT_DIMS)
        for s in range(2):
            spec[c, :, s * 256:(s + 1) * 256] = dot3(
                v_even[s, 0], v_even[s, 1], te[s, 0], te[s, 1], NT_DIMS
            )

    def chunk_decay(c, q):
        start = pl.multiple_of(freq_start(row, c) + q * 8, 8)
        col = lam_cols[pl.ds(start, 8), :]
        return jnp.concatenate([decay(lam_rows[l] + col) for l in range(8)], axis=1)

    def stage_c(c):
        for q in range(CK // 8):
            rho = chunk_decay(c, q)
            b = [spec[c, h * CK + q * 8:h * CK + q * 8 + 8, :] for h in range(HOURS)]
            f = b[3] + rho * (b[2] + rho * (b[1] + rho * b[0]))
            g = b[0] + rho * (b[1] + rho * (b[2] + rho * b[3]))
            for l in range(8):
                fg[c, q * 8 + l, 0:8, :] = f[:, l * 128:(l + 1) * 128]
                fg[c, q * 8 + l, 8:16, :] = g[:, l * 128:(l + 1) * 128]
        own[c, tm] = fg[c, tm]

        @pl.loop(1, TM)
        def _(o):
            peer = lax.rem(tm + o, TM)
            pltpu.make_async_remote_copy(
                src_ref=fg.at[c, peer],
                dst_ref=own.at[c, tm],
                send_sem=sem_sf.at[c],
                recv_sem=sem_rf.at[c],
                device_id={"tm": peer},
                device_id_type=MESH,
            ).start()

    def stage_d(c):
        wait_for(own.at[c, pl.ds(0, TM - 1)], sem_rf.at[c])
        start = pl.multiple_of(freq_start(row, c) + (tm // 8) * 8, 8)
        rho = decay(lam_rows[tm % 8] + lam_cols[pl.ds(start, 8), :])
        rho2 = rho * rho
        rho4 = rho2 * rho2
        whole = rho4
        for _ in range(5):
            whole = whole * whole
        zero = jnp.zeros((8, 128), F32)

        def sums(d, carry):
            p, q = carry
            return own[c, d, 0:8, :] + rho4 * p, own[c, TM - 1 - d, 8:16, :] + rho4 * q

        right, left = lax.fori_loop(0, TM, sums, (zero, zero), unroll=8)
        scale = 1.0 / (1.0 - whole * whole)
        p = (left + whole * right) * scale
        q = (right + whole * left) * scale

        def starts(d, carry):
            p, q = carry
            back[c, d, 0:8, :] = p
            back[c, TM - 1 - d, 8:16, :] = q
            return own[c, d, 0:8, :] + rho4 * p, own[c, TM - 1 - d, 8:16, :] + rho4 * q

        lax.fori_loop(0, TM, starts, (p, q), unroll=8)
        inc[c, tm] = back[c, tm]

        @pl.loop(1, TM)
        def _(o):
            peer = lax.rem(tm + o, TM)
            pltpu.make_async_remote_copy(
                src_ref=back.at[c, peer],
                dst_ref=inc.at[c, tm],
                send_sem=sem_sb.at[c],
                recv_sem=sem_rb.at[c],
                device_id={"tm": peer},
                device_id_type=MESH,
            ).start()

    def stage_e(c):
        wait_for(inc.at[c, pl.ds(0, TM - 1)], sem_rb.at[c])
        for q in range(CK // 8):
            rho = chunk_decay(c, q)
            f = jnp.concatenate([inc[c, q * 8 + l, 0:8, :] for l in range(8)], axis=1)
            g = jnp.concatenate([inc[c, q * 8 + l, 8:16, :] for l in range(8)], axis=1)
            scale = rho / (1.0 - rho * rho) * (1.0 / float(N * N))
            b = [spec[c, h * CK + q * 8:h * CK + q * 8 + 8, :] for h in range(HOURS)]
            later = [None] * HOURS
            g = rho * g
            for h in range(HOURS - 1, -1, -1):
                later[h] = g
                if h:
                    g = rho * (b[h] + g)
            for h in range(HOURS):
                f = b[h] + rho * f
                spec[c, h * CK + q * 8:h * CK + q * 8 + 8, :] = scale * (f + later[h])

    def stage_f(c):
        hi, lo = split(spec[c, :, 512:1024])
        odd = dot3(hi, lo, to[0], to[1], NN)
        parts = []
        for s in range(2):
            hi, lo = split(spec[c, :, s * 256:(s + 1) * 256])
            parts.append(dot3(hi, lo, te[s, 0], te[s, 1], NN))
        even = jnp.concatenate([parts[0] + parts[1], parts[0] - parts[1]], axis=1)
        for half, value in ((0, even + odd), (1, even - odd)):
            for r in range(4):
                for h in range(HOURS):
                    send_w[c, 4 * half + r, :, h * BAND:(h + 1) * BAND] = value[
                        h * CK:(h + 1) * CK, r * BAND:(r + 1) * BAND
                    ]
        here = pl.ds(freq_start(row, c), CK)
        y[here, :] = send_w[c, row]

        @pl.loop(1, ROWS)
        def _(o):
            peer = lax.rem(row + o, ROWS)
            pltpu.make_async_remote_copy(
                src_ref=send_w.at[c, peer],
                dst_ref=y.at[here, :],
                send_sem=sem_sw.at[c],
                recv_sem=sem_rw.at[c],
                device_id={"row": peer},
                device_id_type=MESH,
            ).start()

    @pl.loop(0, CHUNKS)
    def _(c):
        stage_a(c)

    @pl.loop(0, CHUNKS + 2)
    def _(i):
        @pl.when(i < CHUNKS)
        def _():
            stage_b(i)
            stage_c(i)

        @pl.when((i >= 1) & (i < CHUNKS + 1))
        def _():
            stage_d(i - 1)

        @pl.when(i >= 2)
        def _():
            stage_e(i - 2)
            stage_f(i - 2)

    @pl.loop(0, CHUNKS)
    def _(c):
        wait_for(send_a.at[c, pl.ds(0, ROWS - 1)], sem_sa.at[c])
        wait_for(fg.at[c, pl.ds(0, TM - 1)], sem_sf.at[c])
        wait_for(back.at[c, pl.ds(0, TM - 1)], sem_sb.at[c])
        wait_for(send_w.at[c, pl.ds(0, ROWS - 1)], sem_sw.at[c])
        wait_for(send_w.at[c, pl.ds(0, ROWS - 1)], sem_rw.at[c])

    for k, halo in enumerate(halos):
        halo.wait_send()
    for k, count in enumerate((ROWS, 8, 4)):
        wait_for(dot_row.at[pl.ds(0, count - 1)], sem_ds.at[k])
    store.wait()


def step(direction, residual, observed, obs_weight, blocks, te, to, lam_rows, lam_cols, previous):
    anywhere = pl.BlockSpec(memory_space=pl.ANY)
    field = (HOURS, BAND, N)
    return pl.pallas_call(
        step_kernel,
        out_shape=(jax.ShapeDtypeStruct((N, FRONT), F32), jax.ShapeDtypeStruct(field, F32)),
        in_specs=[anywhere] * 9 + [pl.BlockSpec(memory_space=pltpu.SMEM)],
        out_specs=(pl.BlockSpec(memory_space=pltpu.VMEM), anywhere),
        scratch_shapes=[
            pltpu.VMEM(field, F32),
            pltpu.VMEM(field, F32),
            pltpu.VMEM(field, jnp.int32),
            pltpu.VMEM((BAND, N), F32),
            pltpu.VMEM((N // BLOCK, N // BLOCK), jnp.int32),
            pltpu.VMEM((2, 2, 256, 256), BF16),
            pltpu.VMEM((2, 512, 512), BF16),
            pltpu.VMEM((8, 8, 128), F32),
            pltpu.VMEM((N, 128), F32),
            pltpu.VMEM(field, F32),
            pltpu.VMEM((2, BAND, N), F32),
            pltpu.VMEM((2, HOURS, 8, N), F32),
            pltpu.VMEM((N // BLOCK + 16, N), F32),
            pltpu.VMEM((3, 8, 128), F32),
            pltpu.VMEM((8, 8, 128), F32),
            pltpu.VMEM((8, 8, 128), F32),
            pltpu.VMEM((4, 8, 128), F32),
            pltpu.VMEM((2, 2, FRONT, 256), BF16),
            pltpu.VMEM((2, FRONT, 512), BF16),
            pltpu.VMEM((2, 2, M, 256), BF16),
            pltpu.VMEM((2, M, 512), BF16),
            pltpu.VMEM((CHUNKS, ROWS, CK, FRONT), F32),
            pltpu.VMEM((CHUNKS, ROWS, CK, FRONT), F32),
            pltpu.VMEM((CHUNKS, M, N), F32),
            pltpu.VMEM((CHUNKS, TM, 16, 128), F32),
            pltpu.VMEM((CHUNKS, TM, 16, 128), F32),
            pltpu.VMEM((CHUNKS, TM, 16, 128), F32),
            pltpu.VMEM((CHUNKS, TM, 16, 128), F32),
            pltpu.VMEM((CHUNKS, ROWS, CK, FRONT), F32),
            pltpu.SemaphoreType.DMA((9,)),
            pltpu.SemaphoreType.DMA((1,)),
            pltpu.SemaphoreType.DMA((4,)),
            pltpu.SemaphoreType.DMA((4,)),
            pltpu.SemaphoreType.DMA((3,)),
            pltpu.SemaphoreType.DMA((3,)),
        ]
        + [pltpu.SemaphoreType.DMA((CHUNKS,))] * 8,
        compiler_params=pltpu.CompilerParams(
            collective_id=1, has_side_effects=True, vmem_limit_bytes=60 * 1024 * 1024
        ),
        name="step",
    )(direction, residual, observed, obs_weight, blocks, te, to, lam_rows, lam_cols, previous)


def finish_kernel(y, te, to, out):
    value = y[...].T
    hi, lo = split(value[:, 512:1024])
    odd = dot3(hi, lo, to[0], to[1], NN)
    parts = []
    for s in range(2):
        hi, lo = split(value[:, s * 256:(s + 1) * 256])
        parts.append(dot3(hi, lo, te[s, 0], te[s, 1], NN))
    even = jnp.concatenate([parts[0] + parts[1], parts[0] - parts[1]], axis=1)
    out[0, :, 0:512] = even + odd
    out[0, :, 512:1024] = even - odd


def finish(y, te, to):
    return pl.pallas_call(
        finish_kernel,
        grid=(HOURS,),
        out_shape=jax.ShapeDtypeStruct((HOURS, BAND, N), F32),
        in_specs=[
            pl.BlockSpec((N, BAND), lambda h: (0, h)),
            pl.BlockSpec((2, 2, 256, 256), lambda h: (0, 0, 0, 0)),
            pl.BlockSpec((2, 512, 512), lambda h: (0, 0, 0)),
        ],
        out_specs=pl.BlockSpec((1, BAND, N), lambda h: (h, 0, 0)),
        compiler_params=pltpu.CompilerParams(vmem_limit_bytes=48 * 1024 * 1024),
        name="finish",
    )(y, te, to)


def per_device(residual, direction, observed, obs_weight, ocean_blocks, previous_dot):
    te, to, lam_rows, lam_cols = (jnp.asarray(t) for t in tables())
    y, residual_new = step(
        direction, residual, observed, obs_weight, ocean_blocks, te, to, lam_rows, lam_cols,
        previous_dot,
    )
    return (residual_new, finish(y, te, to))


def solution(mesh):
    in_specs = (
        P("tm", "row", None),
        P("tm", "row", None),
        P("tm", "row", None),
        P("row", None),
        P(),
        P(),
    )
    out_specs = (P("tm", "row", None), P("tm", "row", None))
    return jax.shard_map(
        per_device, mesh=mesh, in_specs=in_specs, out_specs=out_specs, check_vma=False
    )
```

```python
import math

import jax
import jax.numpy as jnp
import ml_dtypes
import numpy as np
from jax import lax
from jax.experimental import pallas as pl
from jax.experimental.pallas import tpu as pltpu
from jax.sharding import PartitionSpec as P

MESH = pl.DeviceIdType.MESH
BF16 = jnp.bfloat16
F32 = jnp.float32

BLOCK = 8
NUGGET = 0.25
COUPLING = 50.0
PRECOND_SHIFT = 0.5

N = 1024
NT = 128
ROWS = 8
TM = 32
HOURS = NT // TM
BAND = N // ROWS
CHUNKS = 4
CK = BAND // CHUNKS
M = HOURS * CK
FRONT = HOURS * BAND

NN = (((1,), (0,)), ((), ()))
NT_DIMS = (((1,), (1,)), ((), ()))


def split_np(table):
    high = table.astype(ml_dtypes.bfloat16)
    low = (table - high.astype(np.float64)).astype(ml_dtypes.bfloat16)
    return np.stack([high, low])


def tables():
    def cas(freq, count):
        phase = (freq[:, None] * np.arange(count)[None, :]) % N
        angle = phase * (2.0 * math.pi / N)
        return np.cos(angle) + np.sin(angle)

    four = 4 * np.arange(N // 4)
    two = four + 2
    odd = 2 * np.arange(N // 2) + 1
    even_table = np.stack([split_np(cas(four, N // 4)), split_np(cas(two, N // 4))])
    odd_table = split_np(cas(odd, N // 2))
    order = np.concatenate([four, two, odd])
    lam = (2.0 - 2.0 * np.cos(order * (2.0 * math.pi / N))).astype(np.float32)
    lam_rows = np.broadcast_to(lam.reshape(8, 1, 128), (8, 8, 128)).copy()
    lam_cols = np.broadcast_to(lam[:, None], (N, 128)).copy()
    return even_table, odd_table, lam_rows, lam_cols


def dot3(a_hi, a_lo, b_hi, b_lo, dims):
    def one(a, b):
        return lax.dot_general(a, b, dims, preferred_element_type=F32)

    return one(a_hi, b_hi) + (one(a_hi, b_lo) + one(a_lo, b_hi))


def split(value):
    high = value.astype(BF16)
    low = (value - high.astype(F32)).astype(BF16)
    return high, low


def decay(eigen):
    a = (PRECOND_SHIFT + eigen) * (1.0 / COUPLING)
    root = jnp.sqrt(a * a + 4.0 * a)
    return 2.0 / (a + 2.0 + root)


def freq_start(row, chunk):
    odd = row // 4
    even = 1 - odd
    half = (row // 2) % 2
    start = odd * (512 + chunk * (4 * CK) + (row - 4) * CK) + even * (
        half * 256 + chunk * (2 * CK) + (row % 2) * CK
    )
    return pl.multiple_of(start, CK)


def step_kernel(
    direction, residual, observed, obs_weight, blocks, te_in, to_in, lam_rows_in, lam_cols_in, previous,
    y, res_out,
    dir_v, res_v, obs_v, wgt_v, blk_v, te, to, lam_rows, lam_cols,
    image, halo_t, halo_r, ocean, dots, dot_row, dot_tm,
    r_even, r_odd, v_even, v_odd, send_r, recv_r, send_a, recv_a, spec, fg, own, back, inc, send_w,
    sem_in, sem_out, sem_hs, sem_hr, sem_ds, sem_dr, sem_sr, sem_rr,
    sem_sa, sem_ra, sem_sf, sem_rf, sem_sb, sem_rb, sem_sw, sem_rw,
):
    row = lax.axis_index("row")
    tm = lax.axis_index("tm")
    loads = [
        pltpu.make_async_copy(src, dst, sem_in.at[k])
        for k, (src, dst) in enumerate((
            (blocks, blk_v), (direction, dir_v), (obs_weight, wgt_v), (observed, obs_v),
            (residual, res_v), (te_in, te), (to_in, to), (lam_rows_in, lam_rows),
            (lam_cols_in, lam_cols),
        ))
    ]
    for load in loads:
        load.start()

    barrier = pltpu.get_barrier_semaphore()

    @pl.loop(1, ROWS)
    def _(o):
        pl.semaphore_signal(
            barrier, inc=1, device_id={"row": lax.rem(row + o, ROWS)}, device_id_type=MESH
        )

    @pl.loop(1, TM)
    def _(o):
        pl.semaphore_signal(
            barrier, inc=1, device_id={"tm": lax.rem(tm + o, TM)}, device_id_type=MESH
        )

    def remote(src, dst, send_sem, recv_sem, axis, peer):
        return pltpu.make_async_remote_copy(
            src_ref=src, dst_ref=dst, send_sem=send_sem, recv_sem=recv_sem,
            device_id={axis: peer}, device_id_type=MESH,
        )

    def wait_for(ref, sem):
        pltpu.make_async_copy(ref, ref, sem).wait()

    pl.semaphore_wait(barrier, ROWS - 1 + TM - 1)
    tm_next, tm_prev = lax.rem(tm + 1, TM), lax.rem(tm + TM - 1, TM)
    row_next, row_prev = lax.rem(row + 1, ROWS), lax.rem(row + ROWS - 1, ROWS)
    half = BAND // 2

    def slab(k, hour, start, side, peer):
        rows = pl.ds(start, half)
        return remote(
            direction.at[hour, rows], halo_t.at[side, rows], sem_hs.at[k], sem_hr.at[k], "tm", peer
        )

    halos = [
        remote(
            direction.at[:, pl.ds(BAND - 8, 8), :], halo_r.at[0], sem_hs.at[4], sem_hr.at[4],
            "row", row_next,
        ),
        remote(
            direction.at[:, pl.ds(0, 8), :], halo_r.at[1], sem_hs.at[5], sem_hr.at[5],
            "row", row_prev,
        ),
        slab(0, HOURS - 1, half, 0, tm_next),
        slab(1, 0, 0, 1, tm_prev),
        slab(2, HOURS - 1, 0, 0, tm_next),
        slab(3, 0, half, 1, tm_prev),
    ]
    for halo in halos:
        halo.start()

    loads[0].wait()
    spread = (
        lax.broadcasted_iota(jnp.int32, (N // BLOCK, N), 1) // BLOCK
        == lax.broadcasted_iota(jnp.int32, (N // BLOCK, N), 0)
    ).astype(F32).astype(BF16)
    ocean[0:8, :] = jnp.zeros((8, N), F32)
    ocean[136:144, :] = jnp.zeros((8, N), F32)
    ocean[8:136, :] = lax.dot_general(
        blk_v[...].astype(F32).astype(BF16), spread, NN, preferred_element_type=F32
    )
    def prepare(source):
        for h in range(HOURS):
            @pl.loop(0, BAND // 16)
            def _(i):
                here = pl.ds(pl.multiple_of(i * 16, 16), 16)
                rows = pl.ds(pl.multiple_of(h * BAND + i * 16, 16), 16)
                value = source[h, here, :]
                low = value[:, 0:512]
                high = value[:, 512:1024]
                hi, lo = split(low - high)
                r_odd[0, rows, :] = hi
                r_odd[1, rows, :] = lo
                even = low + high
                for s, part in (
                    (0, even[:, :256] + even[:, 256:]), (1, even[:, :256] - even[:, 256:])
                ):
                    hi, lo = split(part)
                    r_even[s, 0, rows, :] = hi
                    r_even[s, 1, rows, :] = lo

    def columns(c, dest):
        part = pl.ds(pl.multiple_of(c * (4 * CK), 4 * CK), 4 * CK)
        out = dot3(to[0, part, :], to[1, part, :], r_odd[0], r_odd[1], NT_DIMS)
        for r in range(4):
            dest[c, 4 + r] = out[r * CK:(r + 1) * CK]
        part = pl.ds(pl.multiple_of(c * (2 * CK), 2 * CK), 2 * CK)
        for s in range(2):
            out = dot3(
                te[s, 0, part, :], te[s, 1, part, :], r_even[s, 0], r_even[s, 1], NT_DIMS
            )
            for r in range(2):
                dest[c, 2 * s + r] = out[r * CK:(r + 1) * CK]

    def send_columns(source, dest, send_sem, recv_sem):
        dest[row] = source[row]

        @pl.loop(1, ROWS)
        def _(o):
            peer = lax.rem(row + o, ROWS)
            remote(source.at[peer], dest.at[row], send_sem, recv_sem, "row", peer).start()

    for k in (4, 5, 6):
        loads[k].wait()
    prepare(res_v)
    columns(0, send_r)
    send_columns(send_r.at[0], recv_r, sem_sr.at[0], sem_rr.at[0])

    for k in (1, 2, 3):
        loads[k].wait()

    sub = lax.broadcasted_iota(jnp.int32, (8, N), 0)

    def wide(i):
        return jnp.broadcast_to(ocean[pl.ds(row * (BAND // BLOCK) + i + 8, 1), :], (8, N))

    def strip(i, above, below, acc):
        here = pl.ds(pl.multiple_of(i * 8, 8), 8)
        sea, sea_up, sea_down = wide(i), wide(i - 1), wide(i + 1)
        north_link = sea * jnp.where(sub == 0, sea_up, sea)
        south_link = sea * jnp.where(sub == 7, sea_down, sea)
        east_link = sea * pltpu.roll(sea, N - 1, 1)
        sea_weight = sea * wgt_v[here, :]
        v = [dir_v[h, here, :] for h in range(HOURS)]
        for h in range(HOURS):
            north = jnp.where(sub == 0, pltpu.roll(above(h), 1, 0), pltpu.roll(v[h], 1, 0))
            south = jnp.where(sub == 7, pltpu.roll(below(h), 7, 0), pltpu.roll(v[h], 7, 0))
            flux = east_link * (v[h] - pltpu.roll(v[h], N - 1, 1))
            value = (obs_v[h, here, :].astype(F32) * sea_weight + NUGGET) * v[h]
            value += north_link * (v[h] - north) + south_link * (v[h] - south)
            value += flux - pltpu.roll(flux, 1, 1)
            near = [v[h] - v[k] for k in (h - 1, h + 1) if 0 <= k < HOURS]
            value += COUPLING * (near[0] + near[1] if len(near) == 2 else near[0])
            image[h, here, :] = value
            acc += value * v[h]
        return acc

    def inner(i, acc):
        above = pl.ds(pl.multiple_of(i * 8 - 8, 8), 8)
        below = pl.ds(pl.multiple_of(i * 8 + 8, 8), 8)
        return strip(i, lambda h: dir_v[h, above, :], lambda h: dir_v[h, below, :], acc)

    strips = BAND // 8
    acc = lax.fori_loop(1, strips - 1, inner, jnp.zeros((8, N), F32))
    wait_for(halo_r.at[0], sem_hr.at[4])
    acc = strip(0, lambda h: halo_r[0, h], lambda h: dir_v[h, 8:16, :], acc)
    wait_for(halo_r.at[1], sem_hr.at[5])
    acc = strip(
        strips - 1, lambda h: dir_v[h, BAND - 16:BAND - 8, :], lambda h: halo_r[1, h], acc
    )

    @pl.loop(1, CHUNKS)
    def _(c):
        columns(c, send_r)

    hour_links = (
        jnp.full((8, N), jnp.where(tm > 0, COUPLING, 0.0), F32),
        jnp.full((8, N), jnp.where(tm < TM - 1, COUPLING, 0.0), F32),
    )
    for side, start in ((0, half), (1, 0)):
        wait_for(halo_t.at[side, pl.ds(start, half)], sem_hr.at[side])

        def across(i, acc, side=side, start=start):
            here = pl.ds(pl.multiple_of(start + i * 8, 8), 8)
            jump = dir_v[side * (HOURS - 1), here, :] - halo_t[side, here, :]
            return acc + hour_links[side] * (jump * jump)

        acc = lax.fori_loop(0, half // 8, across, acc)

    tile = acc[:, 0:128]
    for l in range(1, 8):
        tile += acc[:, l * 128:(l + 1) * 128]

    def share(tile, k, buf, count, me, axis):
        dots[k] = tile
        buf[me] = tile

        @pl.loop(1, count)
        def _(o):
            peer = lax.rem(me + o, count)
            remote(dots.at[k], buf.at[me], sem_ds.at[k], sem_dr.at[k], axis, peer).start()

    def gather(k, buf, count):
        wait_for(buf.at[pl.ds(0, count - 1)], sem_dr.at[k])
        total = buf[0]
        for j in range(1, count):
            total += buf[j]
        return total

    share(tile, 0, dot_row, ROWS, row, "row")
    for side, start in ((0, 0), (1, half)):
        wait_for(halo_t.at[side, pl.ds(start, half)], sem_hr.at[2 + side])

    @pl.loop(0, strips)
    def _(i):
        here = pl.ds(pl.multiple_of(i * 8, 8), 8)
        for side, h in ((0, 0), (1, HOURS - 1)):
            image[h, here, :] += hour_links[side] * (dir_v[h, here, :] - halo_t[side, here, :])

    share(gather(0, dot_row, ROWS), 1, dot_tm, TM, tm, "tm")
    prepare(image)
    columns(0, send_a)
    send_columns(send_a.at[0], recv_a.at[0], sem_sa.at[0], sem_ra.at[0])

    @pl.loop(1, CHUNKS)
    def _(c):
        columns(c, send_a)

    tile = gather(1, dot_tm, TM)
    total = jnp.sum(jnp.sum(tile, axis=1, keepdims=True), axis=0, keepdims=True)
    alpha = previous[0] / (total / float(NT * N * N))

    @pl.loop(1, CHUNKS)
    def _(c):
        for r in range(ROWS):
            send_a[c, r] = send_r[c, r] - alpha * send_a[c, r]
        send_columns(send_a.at[c], recv_a.at[c], sem_sa.at[c], sem_ra.at[c])

    @pl.loop(0, strips)
    def _(i):
        here = pl.ds(pl.multiple_of(i * 8, 8), 8)
        for h in range(HOURS):
            image[h, here, :] = res_v[h, here, :] - alpha * image[h, here, :]

    store = pltpu.make_async_copy(image, res_out, sem_out.at[0])
    store.start()
    for k in (7, 8):
        loads[k].wait()
    wait_for(recv_r.at[pl.ds(0, ROWS - 1)], sem_rr.at[0])
    wait_for(recv_a.at[0, pl.ds(0, ROWS - 1)], sem_ra.at[0])
    for r in range(ROWS):
        recv_a[0, r] = recv_r[r] - alpha * recv_a[0, r]

    def stage_b(c):
        @pl.when(c > 0)
        def _():
            wait_for(recv_a.at[c, pl.ds(0, ROWS - 1)], sem_ra.at[c])

        for h in range(HOURS):
            rows = slice(h * CK, (h + 1) * CK)
            lanes = slice(h * BAND, (h + 1) * BAND)
            v = [recv_a[c, r, :, lanes] for r in range(ROWS)]
            e = [v[r] + v[r + 4] for r in range(4)]
            for r in range(4):
                hi, lo = split(v[r] - v[r + 4])
                v_odd[0, rows, r * BAND:(r + 1) * BAND] = hi
                v_odd[1, rows, r * BAND:(r + 1) * BAND] = lo
            for r in range(2):
                for s, value in ((0, e[r] + e[r + 2]), (1, e[r] - e[r + 2])):
                    hi, lo = split(value)
                    v_even[s, 0, rows, r * BAND:(r + 1) * BAND] = hi
                    v_even[s, 1, rows, r * BAND:(r + 1) * BAND] = lo
        spec[c, :, 512:1024] = dot3(v_odd[0], v_odd[1], to[0], to[1], NT_DIMS)
        for s in range(2):
            spec[c, :, s * 256:(s + 1) * 256] = dot3(
                v_even[s, 0], v_even[s, 1], te[s, 0], te[s, 1], NT_DIMS
            )

    def chunk_decay(c, q):
        start = pl.multiple_of(freq_start(row, c) + q * 8, 8)
        col = lam_cols[pl.ds(start, 8), :]
        return jnp.concatenate([decay(lam_rows[l] + col) for l in range(8)], axis=1)

    def stage_c(c):
        for q in range(CK // 8):
            rho = chunk_decay(c, q)
            b = [spec[c, h * CK + q * 8:h * CK + q * 8 + 8, :] for h in range(HOURS)]
            f = b[3] + rho * (b[2] + rho * (b[1] + rho * b[0]))
            g = b[0] + rho * (b[1] + rho * (b[2] + rho * b[3]))
            for l in range(8):
                fg[c, q * 8 + l, 0:8, :] = f[:, l * 128:(l + 1) * 128]
                fg[c, q * 8 + l, 8:16, :] = g[:, l * 128:(l + 1) * 128]
        own[c, tm] = fg[c, tm]

        @pl.loop(1, TM)
        def _(o):
            peer = lax.rem(tm + o, TM)
            pltpu.make_async_remote_copy(
                src_ref=fg.at[c, peer],
                dst_ref=own.at[c, tm],
                send_sem=sem_sf.at[c],
                recv_sem=sem_rf.at[c],
                device_id={"tm": peer},
                device_id_type=MESH,
            ).start()

    def stage_d(c):
        wait_for(own.at[c, pl.ds(0, TM - 1)], sem_rf.at[c])
        start = pl.multiple_of(freq_start(row, c) + (tm // 8) * 8, 8)
        rho = decay(lam_rows[tm % 8] + lam_cols[pl.ds(start, 8), :])
        rho2 = rho * rho
        rho4 = rho2 * rho2
        whole = rho4
        for _ in range(5):
            whole = whole * whole
        zero = jnp.zeros((8, 128), F32)

        def sums(d, carry):
            p, q = carry
            return own[c, d, 0:8, :] + rho4 * p, own[c, TM - 1 - d, 8:16, :] + rho4 * q

        right, left = lax.fori_loop(0, TM, sums, (zero, zero), unroll=8)
        scale = 1.0 / (1.0 - whole * whole)
        p = (left + whole * right) * scale
        q = (right + whole * left) * scale

        def starts(d, carry):
            p, q = carry
            back[c, d, 0:8, :] = p
            back[c, TM - 1 - d, 8:16, :] = q
            return own[c, d, 0:8, :] + rho4 * p, own[c, TM - 1 - d, 8:16, :] + rho4 * q

        lax.fori_loop(0, TM, starts, (p, q), unroll=8)
        inc[c, tm] = back[c, tm]

        @pl.loop(1, TM)
        def _(o):
            peer = lax.rem(tm + o, TM)
            pltpu.make_async_remote_copy(
                src_ref=back.at[c, peer],
                dst_ref=inc.at[c, tm],
                send_sem=sem_sb.at[c],
                recv_sem=sem_rb.at[c],
                device_id={"tm": peer},
                device_id_type=MESH,
            ).start()

    def stage_e(c):
        wait_for(inc.at[c, pl.ds(0, TM - 1)], sem_rb.at[c])
        for q in range(CK // 8):
            rho = chunk_decay(c, q)
            f = jnp.concatenate([inc[c, q * 8 + l, 0:8, :] for l in range(8)], axis=1)
            g = jnp.concatenate([inc[c, q * 8 + l, 8:16, :] for l in range(8)], axis=1)
            scale = rho / (1.0 - rho * rho) * (1.0 / float(N * N))
            b = [spec[c, h * CK + q * 8:h * CK + q * 8 + 8, :] for h in range(HOURS)]
            later = [None] * HOURS
            g = rho * g
            for h in range(HOURS - 1, -1, -1):
                later[h] = g
                if h:
                    g = rho * (b[h] + g)
            for h in range(HOURS):
                f = b[h] + rho * f
                spec[c, h * CK + q * 8:h * CK + q * 8 + 8, :] = scale * (f + later[h])

    def stage_f(c):
        hi, lo = split(spec[c, :, 512:1024])
        odd = dot3(hi, lo, to[0], to[1], NN)
        parts = []
        for s in range(2):
            hi, lo = split(spec[c, :, s * 256:(s + 1) * 256])
            parts.append(dot3(hi, lo, te[s, 0], te[s, 1], NN))
        even = jnp.concatenate([parts[0] + parts[1], parts[0] - parts[1]], axis=1)
        for half, value in ((0, even + odd), (1, even - odd)):
            for r in range(4):
                for h in range(HOURS):
                    send_w[c, 4 * half + r, :, h * BAND:(h + 1) * BAND] = value[
                        h * CK:(h + 1) * CK, r * BAND:(r + 1) * BAND
                    ]
        here = pl.ds(freq_start(row, c), CK)
        y[here, :] = send_w[c, row]

        @pl.loop(1, ROWS)
        def _(o):
            peer = lax.rem(row + o, ROWS)
            pltpu.make_async_remote_copy(
                src_ref=send_w.at[c, peer],
                dst_ref=y.at[here, :],
                send_sem=sem_sw.at[c],
                recv_sem=sem_rw.at[c],
                device_id={"row": peer},
                device_id_type=MESH,
            ).start()

    @pl.loop(0, CHUNKS + 2)
    def _(i):
        @pl.when(i < CHUNKS)
        def _():
            stage_b(i)
            stage_c(i)

        @pl.when((i >= 1) & (i < CHUNKS + 1))
        def _():
            stage_d(i - 1)

        @pl.when(i >= 2)
        def _():
            stage_e(i - 2)
            stage_f(i - 2)

    @pl.loop(0, CHUNKS)
    def _(c):
        wait_for(send_a.at[c, pl.ds(0, ROWS - 1)], sem_sa.at[c])
        wait_for(fg.at[c, pl.ds(0, TM - 1)], sem_sf.at[c])
        wait_for(back.at[c, pl.ds(0, TM - 1)], sem_sb.at[c])
        wait_for(send_w.at[c, pl.ds(0, ROWS - 1)], sem_sw.at[c])
        wait_for(send_w.at[c, pl.ds(0, ROWS - 1)], sem_rw.at[c])

    for k, halo in enumerate(halos):
        halo.wait_send()
    wait_for(dot_row.at[pl.ds(0, ROWS - 1)], sem_ds.at[0])
    wait_for(dot_tm.at[pl.ds(0, TM - 1)], sem_ds.at[1])
    wait_for(send_r.at[0, pl.ds(0, ROWS - 1)], sem_sr.at[0])
    store.wait()


def step(direction, residual, observed, obs_weight, blocks, te, to, lam_rows, lam_cols, previous):
    anywhere = pl.BlockSpec(memory_space=pl.ANY)
    field = (HOURS, BAND, N)
    return pl.pallas_call(
        step_kernel,
        out_shape=(jax.ShapeDtypeStruct((N, FRONT), F32), jax.ShapeDtypeStruct(field, F32)),
        in_specs=[anywhere] * 9 + [pl.BlockSpec(memory_space=pltpu.SMEM)],
        out_specs=(pl.BlockSpec(memory_space=pltpu.VMEM), anywhere),
        scratch_shapes=[
            pltpu.VMEM(field, F32),
            pltpu.VMEM(field, F32),
            pltpu.VMEM(field, jnp.int32),
            pltpu.VMEM((BAND, N), F32),
            pltpu.VMEM((N // BLOCK, N // BLOCK), jnp.int32),
            pltpu.VMEM((2, 2, 256, 256), BF16),
            pltpu.VMEM((2, 512, 512), BF16),
            pltpu.VMEM((8, 8, 128), F32),
            pltpu.VMEM((N, 128), F32),
            pltpu.VMEM(field, F32),
            pltpu.VMEM((2, BAND, N), F32),
            pltpu.VMEM((2, HOURS, 8, N), F32),
            pltpu.VMEM((N // BLOCK + 16, N), F32),
            pltpu.VMEM((2, 8, 128), F32),
            pltpu.VMEM((ROWS, 8, 128), F32),
            pltpu.VMEM((TM, 8, 128), F32),
            pltpu.VMEM((2, 2, FRONT, 256), BF16),
            pltpu.VMEM((2, FRONT, 512), BF16),
            pltpu.VMEM((2, 2, M, 256), BF16),
            pltpu.VMEM((2, M, 512), BF16),
            pltpu.VMEM((CHUNKS, ROWS, CK, FRONT), F32),
            pltpu.VMEM((ROWS, CK, FRONT), F32),
            pltpu.VMEM((CHUNKS, ROWS, CK, FRONT), F32),
            pltpu.VMEM((CHUNKS, ROWS, CK, FRONT), F32),
            pltpu.VMEM((CHUNKS, M, N), F32),
            pltpu.VMEM((CHUNKS, TM, 16, 128), F32),
            pltpu.VMEM((CHUNKS, TM, 16, 128), F32),
            pltpu.VMEM((CHUNKS, TM, 16, 128), F32),
            pltpu.VMEM((CHUNKS, TM, 16, 128), F32),
            pltpu.VMEM((CHUNKS, ROWS, CK, FRONT), F32),
            pltpu.SemaphoreType.DMA((9,)),
            pltpu.SemaphoreType.DMA((1,)),
            pltpu.SemaphoreType.DMA((6,)),
            pltpu.SemaphoreType.DMA((6,)),
            pltpu.SemaphoreType.DMA((2,)),
            pltpu.SemaphoreType.DMA((2,)),
            pltpu.SemaphoreType.DMA((1,)),
            pltpu.SemaphoreType.DMA((1,)),
        ]
        + [pltpu.SemaphoreType.DMA((CHUNKS,))] * 8,
        compiler_params=pltpu.CompilerParams(
            collective_id=1, has_side_effects=True, vmem_limit_bytes=60 * 1024 * 1024
        ),
        name="step",
    )(direction, residual, observed, obs_weight, blocks, te, to, lam_rows, lam_cols, previous)


def finish_kernel(y, te, to, out):
    value = y[...].T
    hi, lo = split(value[:, 512:1024])
    odd = dot3(hi, lo, to[0], to[1], NN)
    parts = []
    for s in range(2):
        hi, lo = split(value[:, s * 256:(s + 1) * 256])
        parts.append(dot3(hi, lo, te[s, 0], te[s, 1], NN))
    even = jnp.concatenate([parts[0] + parts[1], parts[0] - parts[1]], axis=1)
    out[0, :, 0:512] = even + odd
    out[0, :, 512:1024] = even - odd


def finish(y, te, to):
    return pl.pallas_call(
        finish_kernel,
        grid=(HOURS,),
        out_shape=jax.ShapeDtypeStruct((HOURS, BAND, N), F32),
        in_specs=[
            pl.BlockSpec((N, BAND), lambda h: (0, h)),
            pl.BlockSpec((2, 2, 256, 256), lambda h: (0, 0, 0, 0)),
            pl.BlockSpec((2, 512, 512), lambda h: (0, 0, 0)),
        ],
        out_specs=pl.BlockSpec((1, BAND, N), lambda h: (h, 0, 0)),
        compiler_params=pltpu.CompilerParams(vmem_limit_bytes=48 * 1024 * 1024),
        name="finish",
    )(y, te, to)


def per_device(residual, direction, observed, obs_weight, ocean_blocks, previous_dot):
    te, to, lam_rows, lam_cols = (jnp.asarray(t) for t in tables())
    y, residual_new = step(
        direction, residual, observed, obs_weight, ocean_blocks, te, to, lam_rows, lam_cols,
        previous_dot,
    )
    return (residual_new, finish(y, te, to))


def solution(mesh):
    in_specs = (
        P("tm", "row", None),
        P("tm", "row", None),
        P("tm", "row", None),
        P("row", None),
        P(),
        P(),
    )
    out_specs = (P("tm", "row", None), P("tm", "row", None))
    return jax.shard_map(
        per_device, mesh=mesh, in_specs=in_specs, out_specs=out_specs, check_vma=False
    )
```

```python
import math

import jax
import jax.numpy as jnp
import ml_dtypes
import numpy as np
from jax import lax
from jax.experimental import pallas as pl
from jax.experimental.pallas import tpu as pltpu
from jax.sharding import PartitionSpec as P

MESH = pl.DeviceIdType.MESH
BF16 = jnp.bfloat16
F32 = jnp.float32

BLOCK = 8
NUGGET = 0.25
COUPLING = 50.0
PRECOND_SHIFT = 0.5

N = 1024
NT = 128
ROWS = 8
TM = 32
HOURS = NT // TM
BAND = N // ROWS
CHUNKS = 4
CK = BAND // CHUNKS
M = HOURS * CK
FRONT = HOURS * BAND

NN = (((1,), (0,)), ((), ()))
NT_DIMS = (((1,), (1,)), ((), ()))


def split_np(table):
    high = table.astype(ml_dtypes.bfloat16)
    low = (table - high.astype(np.float64)).astype(ml_dtypes.bfloat16)
    return np.stack([high, low])


def first_place(row, chunk):
    odd = row // 4
    half = (row // 2) % 2
    return odd * (512 + chunk * (4 * CK) + (row - 4) * CK) + (1 - odd) * (
        half * 256 + chunk * (2 * CK) + (row % 2) * CK
    )


def tables():
    def cas(freq, count):
        phase = (freq[:, None] * np.arange(count)[None, :]) % N
        angle = phase * (2.0 * math.pi / N)
        return np.cos(angle) + np.sin(angle)

    four = 4 * np.arange(N // 4)
    two = four + 2
    odd = 2 * np.arange(N // 2) + 1
    even_table = np.stack([split_np(cas(four, N // 4)), split_np(cas(two, N // 4))])
    odd_table = split_np(cas(odd, N // 2))
    order = np.concatenate([four, two, odd])
    lam = (2.0 - 2.0 * np.cos(order * (2.0 * math.pi / N))).astype(np.float32)
    lam_rows = np.broadcast_to(lam.reshape(8, 1, 128), (8, 8, 128)).copy()
    lam_cols = np.broadcast_to(lam[:, None], (N, 128)).copy()
    places = np.concatenate([
        int(first_place(r, c)) + np.arange(CK) for c in range(CHUNKS) for r in range(ROWS)
    ])
    full_table = split_np(cas(order[places], N)).reshape(2, CHUNKS, ROWS * CK, N)
    return even_table, odd_table, full_table, lam_rows, lam_cols


def dot3(a_hi, a_lo, b_hi, b_lo, dims):
    def one(a, b):
        return lax.dot_general(a, b, dims, preferred_element_type=F32)

    return one(a_hi, b_hi) + (one(a_hi, b_lo) + one(a_lo, b_hi))


def split(value):
    high = value.astype(BF16)
    low = (value - high.astype(F32)).astype(BF16)
    return high, low


def decay(eigen):
    a = (PRECOND_SHIFT + eigen) * (1.0 / COUPLING)
    root = jnp.sqrt(a * a + 4.0 * a)
    return 2.0 / (a + 2.0 + root)


def freq_start(row, chunk):
    return pl.multiple_of(first_place(row, chunk), CK)


def step_kernel(
    direction, residual, observed, obs_weight, blocks, te_in, to_in, tf_in, lam_rows_in, lam_cols_in, previous,
    res_out, pre_out,
    dir_v, res_v, obs_v, wgt_v, blk_v, te, to, tf, lam_rows, lam_cols,
    image, drive, halo_t, halo_r, ocean, dots, dot_row, dot_tm,
    r_even, r_odd, v_even, v_odd, send_r, recv_r, send_a, recv_a, spec, fg, own, back, inc, send_w, recv_w, pre,
    sem_in, sem_out, sem_hs, sem_hr, sem_ds, sem_dr, sem_sr, sem_rr,
    sem_sa, sem_ra, sem_sf, sem_rf, sem_sb, sem_rb, sem_sw, sem_rw,
):
    row = lax.axis_index("row")
    tm = lax.axis_index("tm")
    loads = [
        pltpu.make_async_copy(src, dst, sem_in.at[k])
        for k, (src, dst) in enumerate((
            (blocks, blk_v), (direction, dir_v), (obs_weight, wgt_v), (observed, obs_v),
            (residual, res_v), (te_in, te), (to_in, to), (lam_rows_in, lam_rows),
            (lam_cols_in, lam_cols), (tf_in, tf),
        ))
    ]
    for load in loads:
        load.start()

    barrier = pltpu.get_barrier_semaphore()

    @pl.loop(1, ROWS)
    def _(o):
        pl.semaphore_signal(
            barrier, inc=1, device_id={"row": lax.rem(row + o, ROWS)}, device_id_type=MESH
        )

    @pl.loop(1, TM)
    def _(o):
        pl.semaphore_signal(
            barrier, inc=1, device_id={"tm": lax.rem(tm + o, TM)}, device_id_type=MESH
        )

    def remote(src, dst, send_sem, recv_sem, axis, peer):
        return pltpu.make_async_remote_copy(
            src_ref=src, dst_ref=dst, send_sem=send_sem, recv_sem=recv_sem,
            device_id={axis: peer}, device_id_type=MESH,
        )

    def wait_for(ref, sem):
        pltpu.make_async_copy(ref, ref, sem).wait()

    pl.semaphore_wait(barrier, ROWS - 1 + TM - 1)
    tm_next, tm_prev = lax.rem(tm + 1, TM), lax.rem(tm + TM - 1, TM)
    row_next, row_prev = lax.rem(row + 1, ROWS), lax.rem(row + ROWS - 1, ROWS)
    half = BAND // 2

    def slab(k, hour, start, side, peer):
        rows = pl.ds(start, half)
        return remote(
            direction.at[hour, rows], halo_t.at[side, rows], sem_hs.at[k], sem_hr.at[k], "tm", peer
        )

    halos = [
        remote(
            direction.at[:, pl.ds(BAND - 8, 8), :], halo_r.at[0], sem_hs.at[4], sem_hr.at[4],
            "row", row_next,
        ),
        remote(
            direction.at[:, pl.ds(0, 8), :], halo_r.at[1], sem_hs.at[5], sem_hr.at[5],
            "row", row_prev,
        ),
        slab(0, HOURS - 1, half, 0, tm_next),
        slab(1, 0, 0, 1, tm_prev),
        slab(2, HOURS - 1, 0, 0, tm_next),
        slab(3, 0, half, 1, tm_prev),
    ]
    for halo in halos[:4]:
        halo.start()

    loads[0].wait()
    spread = (
        lax.broadcasted_iota(jnp.int32, (N // BLOCK, N), 1) // BLOCK
        == lax.broadcasted_iota(jnp.int32, (N // BLOCK, N), 0)
    ).astype(F32).astype(BF16)
    ocean[0:8, :] = jnp.zeros((8, N), F32)
    ocean[136:144, :] = jnp.zeros((8, N), F32)
    ocean[8:136, :] = lax.dot_general(
        blk_v[...].astype(F32).astype(BF16), spread, NN, preferred_element_type=F32
    )
    def prepare(source):
        for h in range(HOURS):
            @pl.loop(0, BAND // 16)
            def _(i):
                here = pl.ds(pl.multiple_of(i * 16, 16), 16)
                rows = pl.ds(pl.multiple_of(h * BAND + i * 16, 16), 16)
                value = source[h, here, :]
                low = value[:, 0:512]
                high = value[:, 512:1024]
                hi, lo = split(low - high)
                r_odd[0, rows, :] = hi
                r_odd[1, rows, :] = lo
                even = low + high
                for s, part in (
                    (0, even[:, :256] + even[:, 256:]), (1, even[:, :256] - even[:, 256:])
                ):
                    hi, lo = split(part)
                    r_even[s, 0, rows, :] = hi
                    r_even[s, 1, rows, :] = lo

    def columns(c, dest):
        part = pl.ds(pl.multiple_of(c * (4 * CK), 4 * CK), 4 * CK)
        out = dot3(to[0, part, :], to[1, part, :], r_odd[0], r_odd[1], NT_DIMS)
        for r in range(4):
            dest[c, 4 + r] = out[r * CK:(r + 1) * CK]
        part = pl.ds(pl.multiple_of(c * (2 * CK), 2 * CK), 2 * CK)
        for s in range(2):
            out = dot3(
                te[s, 0, part, :], te[s, 1, part, :], r_even[s, 0], r_even[s, 1], NT_DIMS
            )
            for r in range(2):
                dest[c, 2 * s + r] = out[r * CK:(r + 1) * CK]

    def send_columns(source, dest, send_sem, recv_sem):
        dest[row] = source[row]

        @pl.loop(1, ROWS)
        def _(o):
            peer = lax.rem(row + o, ROWS)
            remote(source.at[peer], dest.at[row], send_sem, recv_sem, "row", peer).start()

    for k in (4, 5, 6):
        loads[k].wait()
    prepare(res_v)
    columns(0, send_r)
    send_columns(send_r.at[0], recv_r, sem_sr.at[0], sem_rr.at[0])

    for k in (1, 2, 3):
        loads[k].wait()

    sub = lax.broadcasted_iota(jnp.int32, (8, N), 0)

    def wide(i):
        return jnp.broadcast_to(ocean[pl.ds(row * (BAND // BLOCK) + i + 8, 1), :], (8, N))

    def strip(i, above, below, acc):
        here = pl.ds(pl.multiple_of(i * 8, 8), 8)
        sea, sea_up, sea_down = wide(i), wide(i - 1), wide(i + 1)
        north_link = sea * jnp.where(sub == 0, sea_up, sea)
        south_link = sea * jnp.where(sub == 7, sea_down, sea)
        east_link = sea * pltpu.roll(sea, N - 1, 1)
        sea_weight = sea * wgt_v[here, :]
        v = [dir_v[h, here, :] for h in range(HOURS)]
        for h in range(HOURS):
            north = jnp.where(sub == 0, pltpu.roll(above(h), 1, 0), pltpu.roll(v[h], 1, 0))
            south = jnp.where(sub == 7, pltpu.roll(below(h), 7, 0), pltpu.roll(v[h], 7, 0))
            north, south, east = v[h] - north, v[h] - south, v[h] - pltpu.roll(v[h], N - 1, 1)
            flux = east_link * east
            value = (obs_v[h, here, :].astype(F32) * sea_weight + NUGGET) * v[h]
            value += north_link * north + south_link * south
            value += flux - pltpu.roll(flux, 1, 1)
            plain = north + south + (east - pltpu.roll(east, 1, 1))
            drive[h, here, :] = value - (PRECOND_SHIFT * v[h] + plain)
            near = [v[h] - v[k] for k in (h - 1, h + 1) if 0 <= k < HOURS]
            value += COUPLING * (near[0] + near[1] if len(near) == 2 else near[0])
            image[h, here, :] = value
            acc += value * v[h]
        return acc

    def inner(i, acc):
        above = pl.ds(pl.multiple_of(i * 8 - 8, 8), 8)
        below = pl.ds(pl.multiple_of(i * 8 + 8, 8), 8)
        return strip(i, lambda h: dir_v[h, above, :], lambda h: dir_v[h, below, :], acc)

    strips = BAND // 8
    acc = lax.fori_loop(1, strips - 1, inner, jnp.zeros((8, N), F32))
    wait_for(halo_r.at[0], sem_hr.at[4])
    acc = strip(0, lambda h: halo_r[0, h], lambda h: dir_v[h, 8:16, :], acc)
    wait_for(halo_r.at[1], sem_hr.at[5])
    acc = strip(
        strips - 1, lambda h: dir_v[h, BAND - 16:BAND - 8, :], lambda h: halo_r[1, h], acc
    )

    hour_links = (
        jnp.full((8, N), jnp.where(tm > 0, COUPLING, 0.0), F32),
        jnp.full((8, N), jnp.where(tm < TM - 1, COUPLING, 0.0), F32),
    )
    for side, start in ((0, half), (1, 0)):
        wait_for(halo_t.at[side, pl.ds(start, half)], sem_hr.at[side])

        def across(i, acc, side=side, start=start):
            here = pl.ds(pl.multiple_of(start + i * 8, 8), 8)
            jump = dir_v[side * (HOURS - 1), here, :] - halo_t[side, here, :]
            return acc + hour_links[side] * (jump * jump)

        acc = lax.fori_loop(0, half // 8, across, acc)

    tile = acc[:, 0:128]
    for l in range(1, 8):
        tile += acc[:, l * 128:(l + 1) * 128]

    def share(tile, k, buf, count, me, axis):
        dots[k] = tile
        buf[me] = tile

        @pl.loop(1, count)
        def _(o):
            peer = lax.rem(me + o, count)
            remote(dots.at[k], buf.at[me], sem_ds.at[k], sem_dr.at[k], axis, peer).start()

    def gather(k, buf, count):
        wait_for(buf.at[pl.ds(0, count - 1)], sem_dr.at[k])
        total = buf[0]
        for j in range(1, count):
            total += buf[j]
        return total

    for halo in halos[4:]:
        halo.start()
    share(tile, 0, dot_row, ROWS, row, "row")

    @pl.loop(1, CHUNKS)
    def _(c):
        columns(c, send_r)

    prepare(drive)
    columns(0, send_a)
    send_columns(send_a.at[0], recv_a.at[0], sem_sa.at[0], sem_ra.at[0])

    share(gather(0, dot_row, ROWS), 1, dot_tm, TM, tm, "tm")

    @pl.loop(1, CHUNKS)
    def _(c):
        columns(c, send_a)

    tile = gather(1, dot_tm, TM)
    total = jnp.sum(jnp.sum(tile, axis=1, keepdims=True), axis=0, keepdims=True)
    alpha = previous[0] / (total / float(NT * N * N))

    def send_rest(c):
        for r in range(ROWS):
            send_a[c, r] = send_r[c, r] - alpha * send_a[c, r]
        send_columns(send_a.at[c], recv_a.at[c], sem_sa.at[c], sem_ra.at[c])

    send_rest(1)
    for k in (7, 8):
        loads[k].wait()
    wait_for(recv_r.at[pl.ds(0, ROWS - 1)], sem_rr.at[0])
    wait_for(recv_a.at[0, pl.ds(0, ROWS - 1)], sem_ra.at[0])
    for r in range(ROWS):
        recv_a[0, r] = recv_r[r] - alpha * recv_a[0, r]

    store = pltpu.make_async_copy(image, res_out, sem_out.at[HOURS])

    def after_first():
        @pl.loop(2, CHUNKS)
        def _(c):
            send_rest(c)

        for side, start in ((0, 0), (1, half)):
            wait_for(halo_t.at[side, pl.ds(start, half)], sem_hr.at[2 + side])

        @pl.loop(0, strips)
        def _(i):
            here = pl.ds(pl.multiple_of(i * 8, 8), 8)
            for side, h in ((0, 0), (1, HOURS - 1)):
                image[h, here, :] += hour_links[side] * (dir_v[h, here, :] - halo_t[side, here, :])

        @pl.loop(0, strips)
        def _(i):
            here = pl.ds(pl.multiple_of(i * 8, 8), 8)
            for h in range(HOURS):
                image[h, here, :] = res_v[h, here, :] - alpha * image[h, here, :]

        store.start()
        loads[9].wait()

    def stage_b(c):
        @pl.when(c > 0)
        def _():
            wait_for(recv_a.at[c, pl.ds(0, ROWS - 1)], sem_ra.at[c])

        for h in range(HOURS):
            rows = slice(h * CK, (h + 1) * CK)
            lanes = slice(h * BAND, (h + 1) * BAND)
            v = [recv_a[c, r, :, lanes] for r in range(ROWS)]
            e = [v[r] + v[r + 4] for r in range(4)]
            for r in range(4):
                hi, lo = split(v[r] - v[r + 4])
                v_odd[0, rows, r * BAND:(r + 1) * BAND] = hi
                v_odd[1, rows, r * BAND:(r + 1) * BAND] = lo
            for r in range(2):
                for s, value in ((0, e[r] + e[r + 2]), (1, e[r] - e[r + 2])):
                    hi, lo = split(value)
                    v_even[s, 0, rows, r * BAND:(r + 1) * BAND] = hi
                    v_even[s, 1, rows, r * BAND:(r + 1) * BAND] = lo
        spec[c, :, 512:1024] = dot3(v_odd[0], v_odd[1], to[0], to[1], NT_DIMS)
        for s in range(2):
            spec[c, :, s * 256:(s + 1) * 256] = dot3(
                v_even[s, 0], v_even[s, 1], te[s, 0], te[s, 1], NT_DIMS
            )

    def chunk_decay(c, q):
        start = pl.multiple_of(freq_start(row, c) + q * 8, 8)
        col = lam_cols[pl.ds(start, 8), :]
        return jnp.concatenate([decay(lam_rows[l] + col) for l in range(8)], axis=1)

    def stage_c(c):
        for q in range(CK // 8):
            rho = chunk_decay(c, q)
            b = [spec[c, h * CK + q * 8:h * CK + q * 8 + 8, :] for h in range(HOURS)]
            f = b[3] + rho * (b[2] + rho * (b[1] + rho * b[0]))
            g = b[0] + rho * (b[1] + rho * (b[2] + rho * b[3]))
            for l in range(8):
                fg[c, q * 8 + l, 0:8, :] = f[:, l * 128:(l + 1) * 128]
                fg[c, q * 8 + l, 8:16, :] = g[:, l * 128:(l + 1) * 128]
        own[c, tm] = fg[c, tm]

        @pl.loop(1, TM)
        def _(o):
            peer = lax.rem(tm + o, TM)
            pltpu.make_async_remote_copy(
                src_ref=fg.at[c, peer],
                dst_ref=own.at[c, tm],
                send_sem=sem_sf.at[c],
                recv_sem=sem_rf.at[c],
                device_id={"tm": peer},
                device_id_type=MESH,
            ).start()

    def stage_d(c):
        wait_for(own.at[c, pl.ds(0, TM - 1)], sem_rf.at[c])
        start = pl.multiple_of(freq_start(row, c) + (tm // 8) * 8, 8)
        rho = decay(lam_rows[tm % 8] + lam_cols[pl.ds(start, 8), :])
        rho2 = rho * rho
        rho4 = rho2 * rho2
        whole = rho4
        for _ in range(5):
            whole = whole * whole
        zero = jnp.zeros((8, 128), F32)

        def sums(d, carry):
            p, q = carry
            return own[c, d, 0:8, :] + rho4 * p, own[c, TM - 1 - d, 8:16, :] + rho4 * q

        right, left = lax.fori_loop(0, TM, sums, (zero, zero), unroll=8)
        scale = 1.0 / (1.0 - whole * whole)
        p = (left + whole * right) * scale
        q = (right + whole * left) * scale

        def starts(d, carry):
            p, q = carry
            back[c, d, 0:8, :] = p
            back[c, TM - 1 - d, 8:16, :] = q
            return own[c, d, 0:8, :] + rho4 * p, own[c, TM - 1 - d, 8:16, :] + rho4 * q

        lax.fori_loop(0, TM, starts, (p, q), unroll=8)
        inc[c, tm] = back[c, tm]

        @pl.loop(1, TM)
        def _(o):
            peer = lax.rem(tm + o, TM)
            pltpu.make_async_remote_copy(
                src_ref=back.at[c, peer],
                dst_ref=inc.at[c, tm],
                send_sem=sem_sb.at[c],
                recv_sem=sem_rb.at[c],
                device_id={"tm": peer},
                device_id_type=MESH,
            ).start()

    def stage_e(c):
        wait_for(inc.at[c, pl.ds(0, TM - 1)], sem_rb.at[c])
        for q in range(CK // 8):
            rho = chunk_decay(c, q)
            f = jnp.concatenate([inc[c, q * 8 + l, 0:8, :] for l in range(8)], axis=1)
            g = jnp.concatenate([inc[c, q * 8 + l, 8:16, :] for l in range(8)], axis=1)
            scale = rho / (1.0 - rho * rho) * (1.0 / float(N * N))
            b = [spec[c, h * CK + q * 8:h * CK + q * 8 + 8, :] for h in range(HOURS)]
            later = [None] * HOURS
            g = rho * g
            for h in range(HOURS - 1, -1, -1):
                later[h] = g
                if h:
                    g = rho * (b[h] + g)
            for h in range(HOURS):
                f = b[h] + rho * f
                spec[c, h * CK + q * 8:h * CK + q * 8 + 8, :] = scale * (f + later[h])

    def stage_f(c):
        hi, lo = split(spec[c, :, 512:1024])
        odd = dot3(hi, lo, to[0], to[1], NN)
        parts = []
        for s in range(2):
            hi, lo = split(spec[c, :, s * 256:(s + 1) * 256])
            parts.append(dot3(hi, lo, te[s, 0], te[s, 1], NN))
        even = jnp.concatenate([parts[0] + parts[1], parts[0] - parts[1]], axis=1)
        for half, value in ((0, even + odd), (1, even - odd)):
            for r in range(4):
                for h in range(HOURS):
                    send_w[c, 4 * half + r, :, h * BAND:(h + 1) * BAND] = value[
                        h * CK:(h + 1) * CK, r * BAND:(r + 1) * BAND
                    ]
        recv_w[c, row] = send_w[c, row]

        @pl.loop(1, ROWS)
        def _(o):
            peer = lax.rem(row + o, ROWS)
            pltpu.make_async_remote_copy(
                src_ref=send_w.at[c, peer],
                dst_ref=recv_w.at[c, row],
                send_sem=sem_sw.at[c],
                recv_sem=sem_rw.at[c],
                device_id={"row": peer},
                device_id_type=MESH,
            ).start()

    def stage_g(c):
        wait_for(recv_w.at[c, pl.ds(0, ROWS - 1)], sem_rw.at[c])
        for h in range(HOURS):
            part = jnp.concatenate(
                [recv_w[c, r, :, h * BAND:(h + 1) * BAND] for r in range(ROWS)], axis=0
            )
            hi, lo = split(part.T)
            out = dot3(hi, lo, tf[0, c], tf[1, c], NN)

            @pl.when(c == 0)
            def _():
                pre[h] = out - (COUPLING * alpha) * dir_v[h]

            @pl.when(c > 0)
            def _():
                pre[h] += out

            @pl.when(c == CHUNKS - 1)
            def _():
                pltpu.make_async_copy(pre.at[h], pre_out.at[h], sem_out.at[h]).start()

    @pl.loop(0, CHUNKS + 3)
    def _(i):
        @pl.when(i < CHUNKS)
        def _():
            stage_b(i)
            stage_c(i)

        @pl.when(i == 0)
        def _():
            after_first()

        @pl.when((i >= 1) & (i < CHUNKS + 1))
        def _():
            stage_d(i - 1)

        @pl.when((i >= 2) & (i < CHUNKS + 2))
        def _():
            stage_e(i - 2)
            stage_f(i - 2)

        @pl.when(i >= 3)
        def _():
            stage_g(i - 3)

    @pl.loop(0, CHUNKS)
    def _(c):
        wait_for(send_a.at[c, pl.ds(0, ROWS - 1)], sem_sa.at[c])
        wait_for(fg.at[c, pl.ds(0, TM - 1)], sem_sf.at[c])
        wait_for(back.at[c, pl.ds(0, TM - 1)], sem_sb.at[c])
        wait_for(send_w.at[c, pl.ds(0, ROWS - 1)], sem_sw.at[c])

    for k, halo in enumerate(halos):
        halo.wait_send()
    wait_for(dot_row.at[pl.ds(0, ROWS - 1)], sem_ds.at[0])
    wait_for(dot_tm.at[pl.ds(0, TM - 1)], sem_ds.at[1])
    wait_for(send_r.at[0, pl.ds(0, ROWS - 1)], sem_sr.at[0])
    store.wait()
    for h in range(HOURS):
        pltpu.make_async_copy(pre.at[h], pre_out.at[h], sem_out.at[h]).wait()


def step(direction, residual, observed, obs_weight, blocks, te, to, tf, lam_rows, lam_cols, previous):
    anywhere = pl.BlockSpec(memory_space=pl.ANY)
    field = (HOURS, BAND, N)
    return pl.pallas_call(
        step_kernel,
        out_shape=(jax.ShapeDtypeStruct(field, F32), jax.ShapeDtypeStruct(field, F32)),
        in_specs=[anywhere] * 10 + [pl.BlockSpec(memory_space=pltpu.SMEM)],
        out_specs=(anywhere, anywhere),
        scratch_shapes=[
            pltpu.VMEM(field, F32),
            pltpu.VMEM(field, F32),
            pltpu.VMEM(field, jnp.int32),
            pltpu.VMEM((BAND, N), F32),
            pltpu.VMEM((N // BLOCK, N // BLOCK), jnp.int32),
            pltpu.VMEM((2, 2, 256, 256), BF16),
            pltpu.VMEM((2, 512, 512), BF16),
            pltpu.VMEM((2, CHUNKS, ROWS * CK, N), BF16),
            pltpu.VMEM((8, 8, 128), F32),
            pltpu.VMEM((N, 128), F32),
            pltpu.VMEM(field, F32),
            pltpu.VMEM(field, F32),
            pltpu.VMEM((2, BAND, N), F32),
            pltpu.VMEM((2, HOURS, 8, N), F32),
            pltpu.VMEM((N // BLOCK + 16, N), F32),
            pltpu.VMEM((2, 8, 128), F32),
            pltpu.VMEM((ROWS, 8, 128), F32),
            pltpu.VMEM((TM, 8, 128), F32),
            pltpu.VMEM((2, 2, FRONT, 256), BF16),
            pltpu.VMEM((2, FRONT, 512), BF16),
            pltpu.VMEM((2, 2, M, 256), BF16),
            pltpu.VMEM((2, M, 512), BF16),
            pltpu.VMEM((CHUNKS, ROWS, CK, FRONT), F32),
            pltpu.VMEM((ROWS, CK, FRONT), F32),
            pltpu.VMEM((CHUNKS, ROWS, CK, FRONT), F32),
            pltpu.VMEM((CHUNKS, ROWS, CK, FRONT), F32),
            pltpu.VMEM((CHUNKS, M, N), F32),
            pltpu.VMEM((CHUNKS, TM, 16, 128), F32),
            pltpu.VMEM((CHUNKS, TM, 16, 128), F32),
            pltpu.VMEM((CHUNKS, TM, 16, 128), F32),
            pltpu.VMEM((CHUNKS, TM, 16, 128), F32),
            pltpu.VMEM((CHUNKS, ROWS, CK, FRONT), F32),
            pltpu.VMEM((CHUNKS, ROWS, CK, FRONT), F32),
            pltpu.VMEM(field, F32),
            pltpu.SemaphoreType.DMA((10,)),
            pltpu.SemaphoreType.DMA((HOURS + 1,)),
            pltpu.SemaphoreType.DMA((6,)),
            pltpu.SemaphoreType.DMA((6,)),
            pltpu.SemaphoreType.DMA((2,)),
            pltpu.SemaphoreType.DMA((2,)),
            pltpu.SemaphoreType.DMA((1,)),
            pltpu.SemaphoreType.DMA((1,)),
        ]
        + [pltpu.SemaphoreType.DMA((CHUNKS,))] * 8,
        compiler_params=pltpu.CompilerParams(
            collective_id=1, has_side_effects=True, vmem_limit_bytes=60 * 1024 * 1024
        ),
        name="step",
    )(direction, residual, observed, obs_weight, blocks, te, to, tf, lam_rows, lam_cols, previous)


def per_device(residual, direction, observed, obs_weight, ocean_blocks, previous_dot):
    te, to, tf, lam_rows, lam_cols = (jnp.asarray(t) for t in tables())
    return step(
        direction, residual, observed, obs_weight, ocean_blocks, te, to, tf, lam_rows, lam_cols,
        previous_dot,
    )


def solution(mesh):
    in_specs = (
        P("tm", "row", None),
        P("tm", "row", None),
        P("tm", "row", None),
        P("row", None),
        P(),
        P(),
    )
    out_specs = (P("tm", "row", None), P("tm", "row", None))
    return jax.shard_map(
        per_device, mesh=mesh, in_specs=in_specs, out_specs=out_specs, check_vma=False
    )
```

```python
import math

import jax
import jax.numpy as jnp
import ml_dtypes
import numpy as np
from jax import lax
from jax.experimental import pallas as pl
from jax.experimental.pallas import tpu as pltpu
from jax.sharding import PartitionSpec as P

MESH = pl.DeviceIdType.MESH
BF16 = jnp.bfloat16
F32 = jnp.float32

BLOCK = 8
NUGGET = 0.25
COUPLING = 50.0
PRECOND_SHIFT = 0.5

N = 1024
NT = 128
ROWS = 8
TM = 32
HOURS = NT // TM
BAND = N // ROWS
CHUNKS = 4
CK = BAND // CHUNKS
M = HOURS * CK
FRONT = HOURS * BAND

NN = (((1,), (0,)), ((), ()))
NT_DIMS = (((1,), (1,)), ((), ()))


def split_np(table):
    high = table.astype(ml_dtypes.bfloat16)
    low = (table - high.astype(np.float64)).astype(ml_dtypes.bfloat16)
    return np.stack([high, low])


def first_place(row, chunk):
    odd = row // 4
    half = (row // 2) % 2
    return odd * (512 + chunk * (4 * CK) + (row - 4) * CK) + (1 - odd) * (
        half * 256 + chunk * (2 * CK) + (row % 2) * CK
    )


def tables():
    def cas(freq, count):
        phase = (freq[:, None] * np.arange(count)[None, :]) % N
        angle = phase * (2.0 * math.pi / N)
        return np.cos(angle) + np.sin(angle)

    four = 4 * np.arange(N // 4)
    two = four + 2
    odd = 2 * np.arange(N // 2) + 1
    even_table = np.stack([split_np(cas(four, N // 4)), split_np(cas(two, N // 4))])
    odd_table = split_np(cas(odd, N // 2))
    order = np.concatenate([four, two, odd])
    lam = (2.0 - 2.0 * np.cos(order * (2.0 * math.pi / N))).astype(np.float32)
    lam_rows = np.broadcast_to(lam.reshape(8, 1, 128), (8, 8, 128)).copy()
    lam_cols = np.broadcast_to(lam[:, None], (N, 128)).copy()
    places = np.concatenate([
        int(first_place(r, c)) + np.arange(CK) for c in range(CHUNKS) for r in range(ROWS)
    ])
    full_table = split_np(cas(order[places], N)).reshape(2, CHUNKS, ROWS * CK, N)
    return even_table, odd_table, full_table, lam_rows, lam_cols


def dot3(a_hi, a_lo, b_hi, b_lo, dims):
    def one(a, b):
        return lax.dot_general(a, b, dims, preferred_element_type=F32)

    return one(a_hi, b_hi) + (one(a_hi, b_lo) + one(a_lo, b_hi))


def split(value):
    high = value.astype(BF16)
    low = (value - high.astype(F32)).astype(BF16)
    return high, low


def decay(eigen):
    a = (PRECOND_SHIFT + eigen) * (1.0 / COUPLING)
    root = jnp.sqrt(a * a + 4.0 * a)
    return 2.0 / (a + 2.0 + root)


def freq_start(row, chunk):
    return pl.multiple_of(first_place(row, chunk), CK)


def step_kernel(
    direction, residual, observed, obs_weight, blocks, te_in, to_in, tf_in, lam_rows_in, lam_cols_in, previous,
    res_out, pre_out,
    dir_v, res_v, obs_v, wgt_v, blk_v, te, to, tf, lam_rows, lam_cols,
    image, drive, halo_t, halo_r, ocean, dots, dot_row, dot_tm,
    r_even, r_odd, v_even, v_odd, d_even, d_odd, send_r, recv_r, send_a, recv_a, spec, fg, own, back, inc, send_w, recv_w, pre,
    sem_in, sem_out, sem_hs, sem_hr, sem_ds, sem_dr, sem_sr, sem_rr,
    sem_sa, sem_ra, sem_sf, sem_rf, sem_sb, sem_rb, sem_sw, sem_rw,
):
    row = lax.axis_index("row")
    tm = lax.axis_index("tm")
    loads = [
        pltpu.make_async_copy(src, dst, sem_in.at[k])
        for k, (src, dst) in enumerate((
            (blocks, blk_v), (direction, dir_v), (obs_weight, wgt_v), (observed, obs_v),
            (residual, res_v), (te_in, te), (to_in, to), (lam_rows_in, lam_rows),
            (lam_cols_in, lam_cols), (tf_in, tf),
        ))
    ]
    for load in loads:
        load.start()

    barrier = pltpu.get_barrier_semaphore()

    @pl.loop(1, ROWS)
    def _(o):
        pl.semaphore_signal(
            barrier, inc=1, device_id={"row": lax.rem(row + o, ROWS)}, device_id_type=MESH
        )

    @pl.loop(1, TM)
    def _(o):
        pl.semaphore_signal(
            barrier, inc=1, device_id={"tm": lax.rem(tm + o, TM)}, device_id_type=MESH
        )

    def remote(src, dst, send_sem, recv_sem, axis, peer):
        return pltpu.make_async_remote_copy(
            src_ref=src, dst_ref=dst, send_sem=send_sem, recv_sem=recv_sem,
            device_id={axis: peer}, device_id_type=MESH,
        )

    def wait_for(ref, sem):
        pltpu.make_async_copy(ref, ref, sem).wait()

    pl.semaphore_wait(barrier, ROWS - 1 + TM - 1)
    tm_next, tm_prev = lax.rem(tm + 1, TM), lax.rem(tm + TM - 1, TM)
    row_next, row_prev = lax.rem(row + 1, ROWS), lax.rem(row + ROWS - 1, ROWS)
    half = BAND // 2

    def slab(k, hour, start, side, peer):
        rows = pl.ds(start, half)
        return remote(
            direction.at[hour, rows], halo_t.at[side, rows], sem_hs.at[k], sem_hr.at[k], "tm", peer
        )

    halos = [
        remote(
            direction.at[:, pl.ds(BAND - 8, 8), :], halo_r.at[0], sem_hs.at[4], sem_hr.at[4],
            "row", row_next,
        ),
        remote(
            direction.at[:, pl.ds(0, 8), :], halo_r.at[1], sem_hs.at[5], sem_hr.at[5],
            "row", row_prev,
        ),
        slab(0, HOURS - 1, half, 0, tm_next),
        slab(1, 0, 0, 1, tm_prev),
        slab(2, HOURS - 1, 0, 0, tm_next),
        slab(3, 0, half, 1, tm_prev),
    ]
    for halo in halos[:4]:
        halo.start()

    loads[0].wait()
    spread = (
        lax.broadcasted_iota(jnp.int32, (N // BLOCK, N), 1) // BLOCK
        == lax.broadcasted_iota(jnp.int32, (N // BLOCK, N), 0)
    ).astype(F32).astype(BF16)
    ocean[0:8, :] = jnp.zeros((8, N), F32)
    ocean[136:144, :] = jnp.zeros((8, N), F32)
    ocean[8:136, :] = lax.dot_general(
        blk_v[...].astype(F32).astype(BF16), spread, NN, preferred_element_type=F32
    )
    def prepare(source, r_even, r_odd):
        for h in range(HOURS):
            @pl.loop(0, BAND // 16)
            def _(i):
                here = pl.ds(pl.multiple_of(i * 16, 16), 16)
                rows = pl.ds(pl.multiple_of(h * BAND + i * 16, 16), 16)
                value = source[h, here, :]
                low = value[:, 0:512]
                high = value[:, 512:1024]
                hi, lo = split(low - high)
                r_odd[0, rows, :] = hi
                r_odd[1, rows, :] = lo
                even = low + high
                for s, part in (
                    (0, even[:, :256] + even[:, 256:]), (1, even[:, :256] - even[:, 256:])
                ):
                    hi, lo = split(part)
                    r_even[s, 0, rows, :] = hi
                    r_even[s, 1, rows, :] = lo

    def columns(c, dest, r_even, r_odd):
        part = pl.ds(pl.multiple_of(c * (4 * CK), 4 * CK), 4 * CK)
        out = dot3(to[0, part, :], to[1, part, :], r_odd[0], r_odd[1], NT_DIMS)
        for r in range(4):
            dest[c, 4 + r] = out[r * CK:(r + 1) * CK]
        part = pl.ds(pl.multiple_of(c * (2 * CK), 2 * CK), 2 * CK)
        for s in range(2):
            out = dot3(
                te[s, 0, part, :], te[s, 1, part, :], r_even[s, 0], r_even[s, 1], NT_DIMS
            )
            for r in range(2):
                dest[c, 2 * s + r] = out[r * CK:(r + 1) * CK]

    def send_columns(source, dest, send_sem, recv_sem):
        dest[row] = source[row]

        @pl.loop(1, ROWS)
        def _(o):
            peer = lax.rem(row + o, ROWS)
            remote(source.at[peer], dest.at[row], send_sem, recv_sem, "row", peer).start()

    for k in (4, 5, 6):
        loads[k].wait()
    prepare(res_v, r_even, r_odd)
    columns(0, send_r, r_even, r_odd)
    send_columns(send_r.at[0], recv_r, sem_sr.at[0], sem_rr.at[0])

    for k in (1, 2, 3):
        loads[k].wait()

    sub = lax.broadcasted_iota(jnp.int32, (8, N), 0)

    def wide(i):
        return jnp.broadcast_to(ocean[pl.ds(row * (BAND // BLOCK) + i + 8, 1), :], (8, N))

    def strip(i, above, below, acc):
        here = pl.ds(pl.multiple_of(i * 8, 8), 8)
        sea, sea_up, sea_down = wide(i), wide(i - 1), wide(i + 1)
        north_link = sea * jnp.where(sub == 0, sea_up, sea)
        south_link = sea * jnp.where(sub == 7, sea_down, sea)
        east_link = sea * pltpu.roll(sea, N - 1, 1)
        sea_weight = sea * wgt_v[here, :]
        v = [dir_v[h, here, :] for h in range(HOURS)]
        for h in range(HOURS):
            north = jnp.where(sub == 0, pltpu.roll(above(h), 1, 0), pltpu.roll(v[h], 1, 0))
            south = jnp.where(sub == 7, pltpu.roll(below(h), 7, 0), pltpu.roll(v[h], 7, 0))
            north, south, east = v[h] - north, v[h] - south, v[h] - pltpu.roll(v[h], N - 1, 1)
            flux = east_link * east
            value = (obs_v[h, here, :].astype(F32) * sea_weight + NUGGET) * v[h]
            value += north_link * north + south_link * south
            value += flux - pltpu.roll(flux, 1, 1)
            plain = north + south + (east - pltpu.roll(east, 1, 1))
            drive[h, here, :] = value - (PRECOND_SHIFT * v[h] + plain)
            near = [v[h] - v[k] for k in (h - 1, h + 1) if 0 <= k < HOURS]
            value += COUPLING * (near[0] + near[1] if len(near) == 2 else near[0])
            image[h, here, :] = value
            acc += value * v[h]
        return acc

    def inner(i, acc):
        above = pl.ds(pl.multiple_of(i * 8 - 8, 8), 8)
        below = pl.ds(pl.multiple_of(i * 8 + 8, 8), 8)
        return strip(i, lambda h: dir_v[h, above, :], lambda h: dir_v[h, below, :], acc)

    strips = BAND // 8
    acc = lax.fori_loop(1, strips - 1, inner, jnp.zeros((8, N), F32))
    wait_for(halo_r.at[0], sem_hr.at[4])
    acc = strip(0, lambda h: halo_r[0, h], lambda h: dir_v[h, 8:16, :], acc)
    wait_for(halo_r.at[1], sem_hr.at[5])
    acc = strip(
        strips - 1, lambda h: dir_v[h, BAND - 16:BAND - 8, :], lambda h: halo_r[1, h], acc
    )

    hour_links = (
        jnp.full((8, N), jnp.where(tm > 0, COUPLING, 0.0), F32),
        jnp.full((8, N), jnp.where(tm < TM - 1, COUPLING, 0.0), F32),
    )
    for side, start in ((0, half), (1, 0)):
        wait_for(halo_t.at[side, pl.ds(start, half)], sem_hr.at[side])

        def across(i, acc, side=side, start=start):
            here = pl.ds(pl.multiple_of(start + i * 8, 8), 8)
            jump = dir_v[side * (HOURS - 1), here, :] - halo_t[side, here, :]
            return acc + hour_links[side] * (jump * jump)

        acc = lax.fori_loop(0, half // 8, across, acc)

    tile = acc[:, 0:128]
    for l in range(1, 8):
        tile += acc[:, l * 128:(l + 1) * 128]

    def share(tile, k, buf, count, me, axis):
        dots[k] = tile
        buf[me] = tile

        @pl.loop(1, count)
        def _(o):
            peer = lax.rem(me + o, count)
            remote(dots.at[k], buf.at[me], sem_ds.at[k], sem_dr.at[k], axis, peer).start()

    def gather(k, buf, count):
        wait_for(buf.at[pl.ds(0, count - 1)], sem_dr.at[k])
        total = buf[0]
        for j in range(1, count):
            total += buf[j]
        return total

    for halo in halos[4:]:
        halo.start()
    share(tile, 0, dot_row, ROWS, row, "row")

    prepare(drive, d_even, d_odd)
    columns(0, send_a, d_even, d_odd)
    send_columns(send_a.at[0], recv_a.at[0], sem_sa.at[0], sem_ra.at[0])

    share(gather(0, dot_row, ROWS), 1, dot_tm, TM, tm, "tm")

    @pl.loop(1, CHUNKS)
    def _(c):
        columns(c, send_r, r_even, r_odd)
        columns(c, send_a, d_even, d_odd)

    tile = gather(1, dot_tm, TM)
    total = jnp.sum(jnp.sum(tile, axis=1, keepdims=True), axis=0, keepdims=True)
    alpha = previous[0] / (total / float(NT * N * N))

    def send_rest(c):
        for r in range(ROWS):
            send_a[c, r] = send_r[c, r] - alpha * send_a[c, r]
        send_columns(send_a.at[c], recv_a.at[c], sem_sa.at[c], sem_ra.at[c])

    send_rest(1)
    for k in (7, 8):
        loads[k].wait()
    wait_for(recv_r.at[pl.ds(0, ROWS - 1)], sem_rr.at[0])
    wait_for(recv_a.at[0, pl.ds(0, ROWS - 1)], sem_ra.at[0])
    for r in range(ROWS):
        recv_a[0, r] = recv_r[r] - alpha * recv_a[0, r]

    store = pltpu.make_async_copy(image, res_out, sem_out.at[HOURS])

    def after_first():
        @pl.loop(2, CHUNKS)
        def _(c):
            send_rest(c)

        for side, start in ((0, 0), (1, half)):
            wait_for(halo_t.at[side, pl.ds(start, half)], sem_hr.at[2 + side])

        @pl.loop(0, strips)
        def _(i):
            here = pl.ds(pl.multiple_of(i * 8, 8), 8)
            for side, h in ((0, 0), (1, HOURS - 1)):
                image[h, here, :] += hour_links[side] * (dir_v[h, here, :] - halo_t[side, here, :])

        @pl.loop(0, strips)
        def _(i):
            here = pl.ds(pl.multiple_of(i * 8, 8), 8)
            for h in range(HOURS):
                image[h, here, :] = res_v[h, here, :] - alpha * image[h, here, :]

        store.start()
        loads[9].wait()

    def stage_b(c):
        @pl.when(c > 0)
        def _():
            wait_for(recv_a.at[c, pl.ds(0, ROWS - 1)], sem_ra.at[c])

        for h in range(HOURS):
            rows = slice(h * CK, (h + 1) * CK)
            lanes = slice(h * BAND, (h + 1) * BAND)
            v = [recv_a[c, r, :, lanes] for r in range(ROWS)]
            e = [v[r] + v[r + 4] for r in range(4)]
            for r in range(4):
                hi, lo = split(v[r] - v[r + 4])
                v_odd[0, rows, r * BAND:(r + 1) * BAND] = hi
                v_odd[1, rows, r * BAND:(r + 1) * BAND] = lo
            for r in range(2):
                for s, value in ((0, e[r] + e[r + 2]), (1, e[r] - e[r + 2])):
                    hi, lo = split(value)
                    v_even[s, 0, rows, r * BAND:(r + 1) * BAND] = hi
                    v_even[s, 1, rows, r * BAND:(r + 1) * BAND] = lo
        spec[c, :, 512:1024] = dot3(v_odd[0], v_odd[1], to[0], to[1], NT_DIMS)
        for s in range(2):
            spec[c, :, s * 256:(s + 1) * 256] = dot3(
                v_even[s, 0], v_even[s, 1], te[s, 0], te[s, 1], NT_DIMS
            )

    def chunk_decay(c, q):
        start = pl.multiple_of(freq_start(row, c) + q * 8, 8)
        col = lam_cols[pl.ds(start, 8), :]
        return jnp.concatenate([decay(lam_rows[l] + col) for l in range(8)], axis=1)

    def stage_c(c):
        for q in range(CK // 8):
            rho = chunk_decay(c, q)
            b = [spec[c, h * CK + q * 8:h * CK + q * 8 + 8, :] for h in range(HOURS)]
            f = b[3] + rho * (b[2] + rho * (b[1] + rho * b[0]))
            g = b[0] + rho * (b[1] + rho * (b[2] + rho * b[3]))
            for l in range(8):
                fg[c, q * 8 + l, 0:8, :] = f[:, l * 128:(l + 1) * 128]
                fg[c, q * 8 + l, 8:16, :] = g[:, l * 128:(l + 1) * 128]
        own[c, tm] = fg[c, tm]

        @pl.loop(1, TM)
        def _(o):
            peer = lax.rem(tm + o, TM)
            pltpu.make_async_remote_copy(
                src_ref=fg.at[c, peer],
                dst_ref=own.at[c, tm],
                send_sem=sem_sf.at[c],
                recv_sem=sem_rf.at[c],
                device_id={"tm": peer},
                device_id_type=MESH,
            ).start()

    def stage_d(c):
        wait_for(own.at[c, pl.ds(0, TM - 1)], sem_rf.at[c])
        start = pl.multiple_of(freq_start(row, c) + (tm // 8) * 8, 8)
        rho = decay(lam_rows[tm % 8] + lam_cols[pl.ds(start, 8), :])
        rho2 = rho * rho
        rho4 = rho2 * rho2
        whole = rho4
        for _ in range(5):
            whole = whole * whole
        zero = jnp.zeros((8, 128), F32)

        def sums(d, carry):
            p, q = carry
            return own[c, d, 0:8, :] + rho4 * p, own[c, TM - 1 - d, 8:16, :] + rho4 * q

        right, left = lax.fori_loop(0, TM, sums, (zero, zero), unroll=8)
        scale = 1.0 / (1.0 - whole * whole)
        p = (left + whole * right) * scale
        q = (right + whole * left) * scale

        def starts(d, carry):
            p, q = carry
            back[c, d, 0:8, :] = p
            back[c, TM - 1 - d, 8:16, :] = q
            return own[c, d, 0:8, :] + rho4 * p, own[c, TM - 1 - d, 8:16, :] + rho4 * q

        lax.fori_loop(0, TM, starts, (p, q), unroll=8)
        inc[c, tm] = back[c, tm]

        @pl.loop(1, TM)
        def _(o):
            peer = lax.rem(tm + o, TM)
            pltpu.make_async_remote_copy(
                src_ref=back.at[c, peer],
                dst_ref=inc.at[c, tm],
                send_sem=sem_sb.at[c],
                recv_sem=sem_rb.at[c],
                device_id={"tm": peer},
                device_id_type=MESH,
            ).start()

    def stage_e(c):
        wait_for(inc.at[c, pl.ds(0, TM - 1)], sem_rb.at[c])
        for q in range(CK // 8):
            rho = chunk_decay(c, q)
            f = jnp.concatenate([inc[c, q * 8 + l, 0:8, :] for l in range(8)], axis=1)
            g = jnp.concatenate([inc[c, q * 8 + l, 8:16, :] for l in range(8)], axis=1)
            scale = rho / (1.0 - rho * rho) * (1.0 / float(N * N))
            b = [spec[c, h * CK + q * 8:h * CK + q * 8 + 8, :] for h in range(HOURS)]
            later = [None] * HOURS
            g = rho * g
            for h in range(HOURS - 1, -1, -1):
                later[h] = g
                if h:
                    g = rho * (b[h] + g)
            for h in range(HOURS):
                f = b[h] + rho * f
                spec[c, h * CK + q * 8:h * CK + q * 8 + 8, :] = scale * (f + later[h])

    def stage_f(c):
        hi, lo = split(spec[c, :, 512:1024])
        odd = dot3(hi, lo, to[0], to[1], NN)
        parts = []
        for s in range(2):
            hi, lo = split(spec[c, :, s * 256:(s + 1) * 256])
            parts.append(dot3(hi, lo, te[s, 0], te[s, 1], NN))
        even = jnp.concatenate([parts[0] + parts[1], parts[0] - parts[1]], axis=1)
        for half, value in ((0, even + odd), (1, even - odd)):
            for r in range(4):
                for h in range(HOURS):
                    send_w[c, 4 * half + r, :, h * BAND:(h + 1) * BAND] = value[
                        h * CK:(h + 1) * CK, r * BAND:(r + 1) * BAND
                    ]
        recv_w[c, row] = send_w[c, row]

        @pl.loop(1, ROWS)
        def _(o):
            peer = lax.rem(row + o, ROWS)
            pltpu.make_async_remote_copy(
                src_ref=send_w.at[c, peer],
                dst_ref=recv_w.at[c, row],
                send_sem=sem_sw.at[c],
                recv_sem=sem_rw.at[c],
                device_id={"row": peer},
                device_id_type=MESH,
            ).start()

    def stage_g(c):
        wait_for(recv_w.at[c, pl.ds(0, ROWS - 1)], sem_rw.at[c])
        for h in range(HOURS):
            part = jnp.concatenate(
                [recv_w[c, r, :, h * BAND:(h + 1) * BAND] for r in range(ROWS)], axis=0
            )
            hi, lo = split(part.T)
            out = dot3(hi, lo, tf[0, c], tf[1, c], NN)

            @pl.when(c == 0)
            def _():
                pre[h] = out - (COUPLING * alpha) * dir_v[h]

            @pl.when(c > 0)
            def _():
                pre[h] += out

            @pl.when(c == CHUNKS - 1)
            def _():
                pltpu.make_async_copy(pre.at[h], pre_out.at[h], sem_out.at[h]).start()

    @pl.loop(0, CHUNKS + 3)
    def _(i):
        @pl.when(i < CHUNKS)
        def _():
            stage_b(i)
            stage_c(i)

        @pl.when(i == 0)
        def _():
            after_first()

        @pl.when((i >= 1) & (i < CHUNKS + 1))
        def _():
            stage_d(i - 1)

        @pl.when((i >= 2) & (i < CHUNKS + 2))
        def _():
            stage_e(i - 2)
            stage_f(i - 2)

        @pl.when(i >= 3)
        def _():
            stage_g(i - 3)

    @pl.loop(0, CHUNKS)
    def _(c):
        wait_for(send_a.at[c, pl.ds(0, ROWS - 1)], sem_sa.at[c])
        wait_for(fg.at[c, pl.ds(0, TM - 1)], sem_sf.at[c])
        wait_for(back.at[c, pl.ds(0, TM - 1)], sem_sb.at[c])
        wait_for(send_w.at[c, pl.ds(0, ROWS - 1)], sem_sw.at[c])

    for k, halo in enumerate(halos):
        halo.wait_send()
    wait_for(dot_row.at[pl.ds(0, ROWS - 1)], sem_ds.at[0])
    wait_for(dot_tm.at[pl.ds(0, TM - 1)], sem_ds.at[1])
    wait_for(send_r.at[0, pl.ds(0, ROWS - 1)], sem_sr.at[0])
    store.wait()
    for h in range(HOURS):
        pltpu.make_async_copy(pre.at[h], pre_out.at[h], sem_out.at[h]).wait()


def step(direction, residual, observed, obs_weight, blocks, te, to, tf, lam_rows, lam_cols, previous):
    anywhere = pl.BlockSpec(memory_space=pl.ANY)
    field = (HOURS, BAND, N)
    return pl.pallas_call(
        step_kernel,
        out_shape=(jax.ShapeDtypeStruct(field, F32), jax.ShapeDtypeStruct(field, F32)),
        in_specs=[anywhere] * 10 + [pl.BlockSpec(memory_space=pltpu.SMEM)],
        out_specs=(anywhere, anywhere),
        scratch_shapes=[
            pltpu.VMEM(field, F32),
            pltpu.VMEM(field, F32),
            pltpu.VMEM(field, jnp.int32),
            pltpu.VMEM((BAND, N), F32),
            pltpu.VMEM((N // BLOCK, N // BLOCK), jnp.int32),
            pltpu.VMEM((2, 2, 256, 256), BF16),
            pltpu.VMEM((2, 512, 512), BF16),
            pltpu.VMEM((2, CHUNKS, ROWS * CK, N), BF16),
            pltpu.VMEM((8, 8, 128), F32),
            pltpu.VMEM((N, 128), F32),
            pltpu.VMEM(field, F32),
            pltpu.VMEM(field, F32),
            pltpu.VMEM((2, BAND, N), F32),
            pltpu.VMEM((2, HOURS, 8, N), F32),
            pltpu.VMEM((N // BLOCK + 16, N), F32),
            pltpu.VMEM((2, 8, 128), F32),
            pltpu.VMEM((ROWS, 8, 128), F32),
            pltpu.VMEM((TM, 8, 128), F32),
            pltpu.VMEM((2, 2, FRONT, 256), BF16),
            pltpu.VMEM((2, FRONT, 512), BF16),
            pltpu.VMEM((2, 2, M, 256), BF16),
            pltpu.VMEM((2, M, 512), BF16),
            pltpu.VMEM((2, 2, FRONT, 256), BF16),
            pltpu.VMEM((2, FRONT, 512), BF16),
            pltpu.VMEM((CHUNKS, ROWS, CK, FRONT), F32),
            pltpu.VMEM((ROWS, CK, FRONT), F32),
            pltpu.VMEM((CHUNKS, ROWS, CK, FRONT), F32),
            pltpu.VMEM((CHUNKS, ROWS, CK, FRONT), F32),
            pltpu.VMEM((CHUNKS, M, N), F32),
            pltpu.VMEM((CHUNKS, TM, 16, 128), F32),
            pltpu.VMEM((CHUNKS, TM, 16, 128), F32),
            pltpu.VMEM((CHUNKS, TM, 16, 128), F32),
            pltpu.VMEM((CHUNKS, TM, 16, 128), F32),
            pltpu.VMEM((CHUNKS, ROWS, CK, FRONT), F32),
            pltpu.VMEM((CHUNKS, ROWS, CK, FRONT), F32),
            pltpu.VMEM(field, F32),
            pltpu.SemaphoreType.DMA((10,)),
            pltpu.SemaphoreType.DMA((HOURS + 1,)),
            pltpu.SemaphoreType.DMA((6,)),
            pltpu.SemaphoreType.DMA((6,)),
            pltpu.SemaphoreType.DMA((2,)),
            pltpu.SemaphoreType.DMA((2,)),
            pltpu.SemaphoreType.DMA((1,)),
            pltpu.SemaphoreType.DMA((1,)),
        ]
        + [pltpu.SemaphoreType.DMA((CHUNKS,))] * 8,
        compiler_params=pltpu.CompilerParams(
            collective_id=1, has_side_effects=True, vmem_limit_bytes=60 * 1024 * 1024
        ),
        name="step",
    )(direction, residual, observed, obs_weight, blocks, te, to, tf, lam_rows, lam_cols, previous)


def per_device(residual, direction, observed, obs_weight, ocean_blocks, previous_dot):
    te, to, tf, lam_rows, lam_cols = (jnp.asarray(t) for t in tables())
    return step(
        direction, residual, observed, obs_weight, ocean_blocks, te, to, tf, lam_rows, lam_cols,
        previous_dot,
    )


def solution(mesh):
    in_specs = (
        P("tm", "row", None),
        P("tm", "row", None),
        P("tm", "row", None),
        P("row", None),
        P(),
        P(),
    )
    out_specs = (P("tm", "row", None), P("tm", "row", None))
    return jax.shard_map(
        per_device, mesh=mesh, in_specs=in_specs, out_specs=out_specs, check_vma=False
    )
```
